128 devices in a mesh: row: 16 (over y, z_lo, core), col: 8 (over x, z_hi).
Axes of the slice: x: 4, y: 4, z: 4 (z_hi: 2, z_lo: 2; z = z_hi * 2 + z_lo), core: 2. Of those that a mesh axis runs over, the one named last changes fastest.
Arguments:
- base_quantized: bfloat16 [1536, 32768], P(('row', 'col')), may hold values from 0 to 4
- base_scales: float32 [1536, 256], P(('row', 'col')), may hold values from 0.08 to 15
- adjusted_quantized: bfloat16 [1536, 32768], P(('row', 'col')), may hold values from 0 to 5.6
- adjusted_scales: float32 [1536, 256], P(('row', 'col')), may hold values from 0.08 to 15
Outputs:
- correlation: bfloat16 [32768, 32768], P('row', 'col')
The draws below stay inside these ranges and needn't reach their ends.
All inputs are finite; a program needn't handle non-finite values.
Results may differ from the reference program's by a relative error of at most 0.0034.
Values may be sent and summed in bfloat16 or wider, within the bound.
A program may use at most 128 MiB of HBM per device.

```python
import math
import jax
import jax.numpy as jnp
from jax import lax

BLK_A = 2048
GROUP = 128
TOKENS = 1536
LATENTS_A = 32768
LATENTS_B = 32768
N_ROW = 16


def shared_levels(key):
    ceiling = jax.random.uniform(jax.random.fold_in(key, 103), (LATENTS_A,), jnp.float32, 1.0, 4.0)
    fractions = jax.random.uniform(jax.random.fold_in(key, 101), (TOKENS, LATENTS_A), jnp.float32, 0.0, 1.0)
    return fractions * ceiling[None, :]


def loudness(key):
    log_level = jax.random.uniform(jax.random.fold_in(key, 202), (TOKENS,), jnp.float32, math.log(0.8), math.log(1.25))
    return jnp.exp(log_level)


def draw_base_quantized(key, part):
    levels = shared_levels(key)
    return levels.astype(jnp.bfloat16)


def draw_adjusted_quantized(key, part):
    levels = shared_levels(key)
    key = jax.random.fold_in(key, 2)
    shuffle = jax.random.permutation(jax.random.fold_in(key, 7), LATENTS_B)
    ceiling = jax.random.uniform(jax.random.fold_in(key, 9), (LATENTS_B,), jnp.float32, 1.0, 4.0)
    fractions = jax.random.uniform(jax.random.fold_in(key, 8), (TOKENS, LATENTS_B), jnp.float32, 0.0, 1.0)
    private = fractions * ceiling[None, :]
    mixed = 0.6 * levels[:, shuffle] + 0.8 * private
    return mixed.astype(jnp.bfloat16)


def block_scales(key, width):
    position = jnp.arange(TOKENS, dtype=jnp.float32) / (TOKENS - 1)
    ranked = jax.random.permutation(jax.random.fold_in(key, 11), width)
    rising = ranked < width // 2
    growth = jnp.where(rising[None, :], 1.0 + 2.0 * position[:, None], 3.0 - 2.0 * position[:, None])
    blocks = jnp.exp(jax.random.uniform(key, (TOKENS, width), jnp.float32, math.log(0.25), math.log(4.0)))
    return blocks * growth


def draw_base_scales(key, part):
    volume = loudness(key)
    key = jax.random.fold_in(key, 3)
    return volume[:, None] * block_scales(key, LATENTS_A // GROUP)


def draw_adjusted_scales(key, part):
    volume = loudness(key)
    key = jax.random.fold_in(key, 4)
    return volume[:, None] * block_scales(key, LATENTS_B // GROUP)


def setup_inputs(seed: int = 0) -> dict:
    key_of = jax.random.split(jax.random.key(seed), 5)
    return {
        "base_quantized": draw_base_quantized(jax.random.fold_in(key_of[4], 71), 0),
        "base_scales": draw_base_scales(jax.random.fold_in(key_of[4], 71), 0),
        "adjusted_quantized": draw_adjusted_quantized(jax.random.fold_in(key_of[4], 71), 0),
        "adjusted_scales": draw_adjusted_scales(jax.random.fold_in(key_of[4], 71), 0),
    }


def dequantize(quantized, scales):
    row_count = quantized.shape[0]
    grouped = quantized.astype(jnp.float32).reshape(row_count, scales.shape[1], -1) * scales[:, :, None]
    return grouped.reshape(row_count, -1)

def standardize(values, column_sum, squares, token_count):
    average = column_sum / token_count
    spread = squares / token_count - average * average
    scaled = (values - average) * lax.rsqrt(spread + 1e-06) * (1.0 / math.sqrt(token_count))
    return scaled.astype(jnp.bfloat16)

def reference(base_quantized, base_scales, adjusted_quantized, adjusted_scales):
    base_values = dequantize(base_quantized, base_scales)
    adjusted_values = dequantize(adjusted_quantized, adjusted_scales)
    base_unit = standardize(base_values, lax.optimization_barrier(jnp.sum(base_values, axis=0)), lax.optimization_barrier(jnp.sum(base_values * base_values, axis=0)), TOKENS)
    adjusted_unit = standardize(adjusted_values, lax.optimization_barrier(jnp.sum(adjusted_values, axis=0)), lax.optimization_barrier(jnp.sum(adjusted_values * adjusted_values, axis=0)), TOKENS)
    blocks = jnp.transpose(base_unit).reshape(N_ROW, BLK_A, TOKENS)

    def one_block(block_rows):
        return jnp.dot(block_rows, adjusted_unit, preferred_element_type=jnp.float32).astype(jnp.bfloat16)
    tiles = lax.map(one_block, blocks)
    return tiles.reshape(LATENTS_A, LATENTS_B)
```

```python
import functools
import math

import jax
import jax.numpy as jnp
from jax import lax
from jax.experimental import pallas as pl
from jax.experimental.pallas import tpu as pltpu
from jax.sharding import PartitionSpec as P

MESH = pl.DeviceIdType.MESH
VMEM = pltpu.VMEM
BF16 = jnp.bfloat16
F32 = jnp.float32

CORES = 2
RING = 4
GROUP = 128
SLOTS = RING * RING
OWNERS = 8
BASE, ADJ = 0, 1
CHUNK = 256
HALF = CHUNK // 2


def place():
    row, col = lax.axis_index("row"), lax.axis_index("col")
    x, z_hi = col // 2, col % 2
    y, z_lo, core = row // 4, (row // 2) % 2, row % 2
    return x, y, z_hi * 2 + z_lo, core


def device(x, y, z, core):
    x, y, z = x % RING, y % RING, z % RING
    return (y * 2 + z % 2) * CORES + core, x * 2 + z // 2


def gather_kernel(
    local, width,
    base_q, base_s, adj_q, adj_s,
    base_t, adj_u,
    peer_q, peer_s, send_q, send_s, raw, raw_s, unit,
    s0_send, s0_recv, s1_send, s1_recv, s2_send, s2_recv, s3_send, s3_recv,
    own_sem, swap_send, swap_recv,
):
    x, y, z, core = place()
    other = 1 - core
    chunks = width // CHUNK
    tokens = adj_u.shape[1]
    token_pair = 4 * local
    queue = (base_q, adj_q)
    scale = (base_s, adj_s)
    peer = device(x, y, z, other)

    def plane(op, slot):
        a, b = slot // RING, slot % RING
        return (x, y + a, z + b) if op == BASE else (x + a, y, z + b)

    def owner(op, slot):
        px, py, pz = plane(op, slot)
        if op == BASE:
            return (py % RING) * 2 + (pz % RING) % 2
        return (px % RING) * 2 + (pz % RING) // 2

    def along(op, step):
        return device(x + step, y, z, core) if op == BASE else device(x, y + step, z, core)

    def landing(op, i):
        return raw_s.at[op] if i == chunks else raw.at[i, op]

    def leaving(op, i):
        return send_s.at[op] if i == chunks else send_q.at[i, op]

    def remote(src, dst, send_sem, recv_sem, where):
        return pltpu.make_async_remote_copy(
            src_ref=src, dst_ref=dst, send_sem=send_sem, recv_sem=recv_sem,
            device_id=where, device_id_type=MESH,
        )

    def wait_for(ref, sem):
        pltpu.make_async_copy(ref, ref, sem).wait()

    barrier = pltpu.get_barrier_semaphore()
    greeted = [peer]
    for slot in range(1, SLOTS):
        greeted.append(device(*plane(BASE, slot), core))
        if slot >= RING:
            greeted.append(device(*plane(ADJ, slot), core))
    for where in greeted:
        pl.semaphore_signal(barrier, inc=1, device_id=where, device_id_type=MESH)
    pl.semaphore_wait(barrier, len(greeted))

    for op in (BASE, ADJ):
        for b in range(OWNERS):
            start = pl.multiple_of((2 * b + other) * width, width)
            remote(
                queue[op].at[:, pl.ds(start, width)], peer_q.at[op, b],
                s0_send.at[op], s0_recv.at[op], peer,
            ).start()
        remote(scale[op], peer_s.at[op], s0_send.at[2 + op], s0_recv.at[2 + op], peer).start()
    for op in (BASE, ADJ):
        wait_for(peer_q.at[op], s0_recv.at[op])
        wait_for(peer_s.at[op], s0_recv.at[2 + op])

    def both_cores(own, theirs):
        own, theirs = own.astype(F32), theirs.astype(F32)
        first = jnp.where(core == 0, own, theirs)
        second = jnp.where(core == 0, theirs, own)
        return jnp.concatenate([first, second], axis=0)

    lanes = lax.broadcasted_iota(jnp.int32, (8, 128), 1)
    per_block = width // GROUP
    subs = CORES * local // 8

    def pack_scales(op):
        all_s = both_cores(scale[op][...], peer_s[op])
        for b in range(OWNERS):
            tile = 2 * b * per_block // 128
            first = (2 * b * per_block) % 128
            packed = jnp.zeros((8, 128), F32)
            for sub in range(subs):
                part = all_s[sub * 8 : sub * 8 + 8, tile * 128 : tile * 128 + 128]
                shift = (sub * per_block + 256 - first - core * per_block) % 128
                part = pltpu.roll(part, shift, 1)
                mine = (lanes >= sub * per_block) & (lanes < (sub + 1) * per_block)
                packed = jnp.where(mine, part, packed)
            send_s[op, b] = packed

    def pack(op, i):
        @pl.loop(0, OWNERS)
        def _(b):
            parts = []
            for h in range(2):
                start = pl.multiple_of((2 * b + core) * width + i * CHUNK + h * HALF, HALF)
                parts.append(
                    both_cores(
                        queue[op][:, pl.ds(start, HALF)],
                        peer_q[op, b, :, pl.ds(i * CHUNK + h * HALF, HALF)],
                    )
                )
            send_q[i, op, b] = jnp.concatenate(parts, axis=0).astype(BF16)

    def scatter(op, i):
        for slot in range(1, SLOTS):
            remote(
                leaving(op, i).at[owner(op, slot)], landing(op, i).at[0, slot],
                s1_send.at[op, i], s1_recv.at[op, i], device(*plane(op, slot), core),
            ).start()
        pltpu.make_async_copy(
            leaving(op, i).at[owner(op, 0)], landing(op, i).at[0, 0], own_sem.at[op, i]
        ).start()

    def spread(op, i):
        wait_for(landing(op, i).at[0, pl.ds(1, SLOTS - 1)], s1_recv.at[op, i])
        wait_for(landing(op, i).at[0, 0], own_sem.at[op, i])
        for d, step in enumerate((1, -1)):
            remote(
                landing(op, i).at[0], landing(op, i).at[step % RING],
                s2_send.at[op, i, d], s2_recv.at[op, i, d], along(op, step),
            ).start()

    def forward(op, i):
        for d, step in enumerate((1, -1)):
            part = pl.ds(d * (SLOTS // 2), SLOTS // 2)
            wait_for(landing(op, i).at[step % RING], s2_recv.at[op, i, d])
            remote(
                landing(op, i).at[step % RING, part], landing(op, i).at[2, part],
                s3_send.at[op, i, d], s3_recv.at[op, i, d], along(op, step),
            ).start()

    def arrived(op, i):
        for d in range(2):
            part = pl.ds(d * (SLOTS // 2), SLOTS // 2)
            wait_for(landing(op, i).at[2, part], s3_recv.at[op, i, d])

    pairs = RING * SLOTS // 2

    def values(op, i, p):
        out = [[], []]
        for q in range(2):
            slot = (p % (SLOTS // 2)) * 2 + q
            block = raw[i, op, p // (SLOTS // 2), slot].astype(F32)
            s = raw_s[op, p // (SLOTS // 2), slot]
            for h in range(2):
                for sub in range(subs):
                    lane = sub * per_block + 2 * i + h
                    r = (h * subs + sub) * 8
                    out[h].append(block[r : r + 8] * s[:, lane : lane + 1])
        return out

    def standardize(op, i):
        def add(p, carry):
            sums, squares = carry
            parts = values(op, i, p)
            sums, squares = list(sums), list(squares)
            for h in range(2):
                for v in parts[h]:
                    sums[h] = sums[h] + v
                    squares[h] = squares[h] + v * v
            return tuple(sums), tuple(squares)

        zero = jnp.zeros((8, HALF), F32)
        sums, squares = lax.fori_loop(0, pairs, add, ((zero, zero), (zero, zero)))
        average, factor = [], []
        for h in range(2):
            a = jnp.sum(sums[h], axis=0, keepdims=True) / tokens
            spread_ = jnp.sum(squares[h], axis=0, keepdims=True) / tokens - a * a
            average.append(jnp.broadcast_to(a, (8, HALF)))
            factor.append(
                jnp.broadcast_to(lax.rsqrt(spread_ + 1e-06) * (1.0 / math.sqrt(tokens)), (8, HALF))
            )

        @pl.loop(0, pairs)
        def _(p):
            parts = values(op, i, p)
            for h in range(2):
                u = jnp.concatenate([(v - average[h]) * factor[h] for v in parts[h]], axis=0)
                column = i * CHUNK + h * HALF
                if op == BASE:
                    start = pl.multiple_of(p * token_pair, token_pair)
                    unit[pl.ds(start, token_pair), h * HALF : (h + 1) * HALF] = u.astype(BF16)
                else:
                    at = ((p % 8) // 2) * 8 + (p // 8) * 2 + p % 2
                    start = pl.multiple_of(at * token_pair, token_pair)
                    adj_u[core, pl.ds(start, token_pair), column : column + HALF] = u.astype(BF16)

    def finish(i):
        column = pl.ds(i * CHUNK, CHUNK)
        arrived(ADJ, i)
        standardize(ADJ, i)
        remote(
            adj_u.at[core, :, column], adj_u.at[core, :, column],
            swap_send.at[i], swap_recv.at[i], peer,
        ).start()
        arrived(BASE, i)
        standardize(BASE, i)

        @pl.loop(0, tokens // 128)
        def _(t):
            start = pl.multiple_of(t * 128, 128)
            base_t[column, pl.ds(start, 128)] = unit[pl.ds(start, 128), :].T

        wait_for(adj_u.at[other, :, column], swap_recv.at[i])

    for op in (BASE, ADJ):
        pack_scales(op)
        scatter(op, chunks)
    for step in range(chunks + 3):
        if step < chunks:
            for op in (BASE, ADJ):
                pack(op, step)
                scatter(op, step)
        i = step - 1
        if 0 <= i < chunks:
            for op in (BASE, ADJ):
                if i == 0:
                    spread(op, chunks)
                spread(op, i)
        i = step - 2
        if 0 <= i < chunks:
            for op in (BASE, ADJ):
                if i == 0:
                    forward(op, chunks)
                forward(op, i)
        i = step - 3
        if 0 <= i < chunks:
            if i == 0:
                arrived(BASE, chunks)
                arrived(ADJ, chunks)
            finish(i)

    for op in (BASE, ADJ):
        wait_for(peer_q.at[op], s0_send.at[op])
        wait_for(peer_s.at[op], s0_send.at[2 + op])
        for i in range(chunks + 1):
            wait_for(landing(op, i).at[0, pl.ds(1, SLOTS - 1)], s1_send.at[op, i])
            for d in range(2):
                wait_for(landing(op, i).at[0], s2_send.at[op, i, d])
                wait_for(landing(op, i).at[0, pl.ds(0, SLOTS // 2)], s3_send.at[op, i, d])
    for i in range(chunks):
        wait_for(adj_u.at[core, :, pl.ds(i * CHUNK, CHUNK)], swap_send.at[i])


def gather(base_q, base_s, adj_q, adj_s):
    local, latents = base_q.shape
    width = latents // (OWNERS * CORES)
    chunks = width // CHUNK
    tokens = local * CORES * RING**3
    rows = 2 * CORES * local
    dma = pltpu.SemaphoreType.DMA
    whole = pl.BlockSpec(memory_space=VMEM)
    return pl.pallas_call(
        functools.partial(gather_kernel, local, width),
        out_shape=(VMEM((width, tokens), BF16), VMEM((CORES, tokens, width), BF16)),
        in_specs=[whole] * 4,
        out_specs=(whole, whole),
        scratch_shapes=[
            VMEM((2, OWNERS, local, width), BF16),
            VMEM((2,) + base_s.shape, F32),
            VMEM((chunks, 2, OWNERS, rows, HALF), BF16),
            VMEM((2, OWNERS, 8, 128), F32),
            VMEM((chunks, 2, RING, SLOTS, rows, HALF), BF16),
            VMEM((2, RING, SLOTS, 8, 128), F32),
            VMEM((tokens, CHUNK), BF16),
            dma((4,)), dma((4,)),
            dma((2, chunks + 1)), dma((2, chunks + 1)),
            dma((2, chunks + 1, 2)), dma((2, chunks + 1, 2)),
            dma((2, chunks + 1, 2)), dma((2, chunks + 1, 2)),
            dma((2, chunks + 1)),
            dma((chunks,)), dma((chunks,)),
        ],
        compiler_params=pltpu.CompilerParams(
            collective_id=0, has_side_effects=True, vmem_limit_bytes=28 << 20
        ),
        name="gather_units",
    )(base_q, base_s, adj_q, adj_s)


TILE_M, TILE_N = 256, 512


def product_kernel(base_t, adj_u, out, stage, sems):
    width = base_t.shape[0]
    per_row = CORES * width // TILE_N
    tiles = (width // TILE_M) * per_row

    def target(t):
        r = pl.multiple_of((t // per_row) * TILE_M, TILE_M)
        c = pl.multiple_of((t % per_row) * TILE_N, TILE_N)
        return out.at[pl.ds(r, TILE_M), pl.ds(c, TILE_N)]

    def copy(t):
        return pltpu.make_async_copy(stage.at[t % 4], target(t), sems.at[t % 4])

    @pl.loop(0, tiles)
    def _(t):
        r = pl.multiple_of((t // per_row) * TILE_M, TILE_M)
        n = t % per_row
        c = pl.multiple_of((n % (per_row // CORES)) * TILE_N, TILE_N)

        @pl.when(t >= 4)
        def _():
            copy(t - 4).wait()

        stage[t % 4] = jnp.dot(
            base_t[pl.ds(r, TILE_M), :],
            adj_u[n // (per_row // CORES), :, pl.ds(c, TILE_N)],
            preferred_element_type=F32,
        ).astype(BF16)
        copy(t).start()

    for t in range(tiles - 4, tiles):
        copy(t).wait()


def product(base_t, adj_u):
    width = base_t.shape[0]
    whole = pl.BlockSpec(memory_space=VMEM)
    return pl.pallas_call(
        product_kernel,
        out_shape=jax.ShapeDtypeStruct((width, CORES * width), BF16),
        in_specs=[whole, whole],
        out_specs=pl.BlockSpec(memory_space=pl.ANY),
        scratch_shapes=[
            VMEM((4, TILE_M, TILE_N), BF16),
            pltpu.SemaphoreType.DMA((4,)),
        ],
        compiler_params=pltpu.CompilerParams(vmem_limit_bytes=8 << 20),
        name="correlate",
    )(base_t, adj_u)


def on_device(base_q, base_s, adj_q, adj_s):
    base_t, adj_u = gather(base_q, base_s, adj_q, adj_s)
    base_t = pltpu.with_memory_space_constraint(base_t, VMEM)
    adj_u = pltpu.with_memory_space_constraint(adj_u, VMEM)
    return product(base_t, adj_u)


def solution(mesh):
    spec = P(("row", "col"), None)
    return jax.shard_map(
        on_device, mesh=mesh, in_specs=(spec,) * 4, out_specs=P("row", "col"), check_vma=False
    )
```

```python
import functools
import math

import jax
import jax.numpy as jnp
from jax import lax
from jax.experimental import pallas as pl
from jax.experimental.pallas import tpu as pltpu
from jax.sharding import PartitionSpec as P

MESH = pl.DeviceIdType.MESH
VMEM = pltpu.VMEM
BF16 = jnp.bfloat16
F32 = jnp.float32

CORES = 2
RING = 4
GROUP = 128
SLOTS = RING * RING
OWNERS = 8
BASE, ADJ = 0, 1
CHUNK = 256
HALF = CHUNK // 2


def place():
    row, col = lax.axis_index("row"), lax.axis_index("col")
    x, z_hi = col // 2, col % 2
    y, z_lo, core = row // 4, (row // 2) % 2, row % 2
    return x, y, z_hi * 2 + z_lo, core


def device(x, y, z, core):
    x, y, z = x % RING, y % RING, z % RING
    return (y * 2 + z % 2) * CORES + core, x * 2 + z // 2


def pieces(n, most):
    count = max(1, -(-n // most))
    edges = [n // CHUNK * j // count * CHUNK for j in range(count + 1)]
    return [(a, b - a) for a, b in zip(edges, edges[1:]) if b > a]


def multiply(base_t, adj_u, below, beside, i, done=None):
    last = done is not None
    new = slice(i * CHUNK, (i + 1) * CHUNK)
    into = slice(0, CHUNK) if last else new

    @pl.loop(0, CORES)
    def _(half):
        for a, n in pieces((i + 1) * CHUNK, 1024):
            below[half, a : a + n, into] = jnp.dot(
                base_t[a : a + n, :], adj_u[half, :, new], preferred_element_type=F32
            ).astype(BF16)
        if last:
            done(half, 0)
        for a, n in pieces(i * CHUNK, 1024):
            beside[half, into, a : a + n] = jnp.dot(
                base_t[new, :], adj_u[half, :, a : a + n], preferred_element_type=F32
            ).astype(BF16)
        if last:
            done(half, 1)


def gather_kernel(
    local, width,
    base_q, base_s, adj_q, adj_s,
    base_t, adj_u, early,
    own_q, own_s, peer_q, peer_s, send_q, send_s, raw, raw_s,
    split_s, pick, wide_s, work,
    load_sem, s0_send, s0_recv, s1_send, s1_recv, s2_send, s2_recv, s3_send, s3_recv,
    own_sem, swap_send, swap_recv,
):
    x, y, z, core = place()
    other = 1 - core
    chunks = width // CHUNK
    tokens = adj_u.shape[1]
    token_ring = CORES * RING * local
    queue = (base_q, adj_q)
    scale = (base_s, adj_s)
    peer = device(x, y, z, other)

    def plane(op, slot):
        a, b = slot // RING, slot % RING
        return (x, y + a, z + b) if op == BASE else (x + a, y, z + b)

    def owner(op, slot):
        px, py, pz = plane(op, slot)
        if op == BASE:
            return (py % RING) * 2 + (pz % RING) % 2
        return (px % RING) * 2 + (pz % RING) // 2

    def along(op, step):
        return device(x + step, y, z, core) if op == BASE else device(x, y + step, z, core)

    def landing(op, i):
        return raw_s.at[op] if i == chunks else raw.at[i, op]

    def leaving(op, i):
        return send_s.at[op] if i == chunks else send_q.at[i, op]

    def remote(src, dst, send_sem, recv_sem, where):
        return pltpu.make_async_remote_copy(
            src_ref=src, dst_ref=dst, send_sem=send_sem, recv_sem=recv_sem,
            device_id=where, device_id_type=MESH,
        )

    def wait_for(ref, sem):
        pltpu.make_async_copy(ref, ref, sem).wait()

    loads = []
    for op in (BASE, ADJ):
        for b in range(OWNERS):
            start = pl.multiple_of((2 * b + core) * width, width)
            loads.append(
                pltpu.make_async_copy(
                    queue[op].at[:, pl.ds(start, width)], own_q.at[op, b], load_sem.at[op, b]
                )
            )
        loads.append(pltpu.make_async_copy(scale[op], own_s.at[op], load_sem.at[op, OWNERS]))
    for load in loads:
        load.start()

    barrier = pltpu.get_barrier_semaphore()
    greeted = [peer]
    for slot in range(1, SLOTS):
        greeted.append(device(*plane(BASE, slot), core))
        if slot >= RING:
            greeted.append(device(*plane(ADJ, slot), core))
    for where in greeted:
        pl.semaphore_signal(barrier, inc=1, device_id=where, device_id_type=MESH)
    pl.semaphore_wait(barrier, len(greeted))

    for op in (BASE, ADJ):
        for b in range(OWNERS):
            start = pl.multiple_of((2 * b + other) * width, width)
            remote(
                queue[op].at[:, pl.ds(start, width)], peer_q.at[op, b],
                s0_send.at[op], s0_recv.at[op], peer,
            ).start()
        remote(scale[op], peer_s.at[op], s0_send.at[2 + op], s0_recv.at[2 + op], peer).start()
    for load in loads:
        load.wait()
    for op in (BASE, ADJ):
        wait_for(peer_q.at[op], s0_recv.at[op])
        wait_for(peer_s.at[op], s0_recv.at[2 + op])

    def both_cores(own, theirs):
        own, theirs = own.astype(F32), theirs.astype(F32)
        first = jnp.where(core == 0, own, theirs)
        second = jnp.where(core == 0, theirs, own)
        return jnp.concatenate([first, second], axis=0)

    lanes = lax.broadcasted_iota(jnp.int32, (8, 128), 1)
    per_block = width // GROUP
    subs = CORES * local // 8

    def pack_scales(op):
        all_s = both_cores(own_s[op], peer_s[op])
        for b in range(OWNERS):
            tile = 2 * b * per_block // 128
            first = (2 * b * per_block) % 128
            packed = jnp.zeros((8, 128), F32)
            for sub in range(subs):
                part = all_s[sub * 8 : sub * 8 + 8, tile * 128 : tile * 128 + 128]
                shift = (sub * per_block + 256 - first - core * per_block) % 128
                part = pltpu.roll(part, shift, 1)
                mine = (lanes >= sub * per_block) & (lanes < (sub + 1) * per_block)
                packed = jnp.where(mine, part, packed)
            send_s[op, b] = packed

    def pack(op, i):
        @pl.loop(0, OWNERS)
        def _(b):
            parts = []
            for h in range(2):
                part = pl.ds(i * CHUNK + h * HALF, HALF)
                parts.append(both_cores(own_q[op, b, :, part], peer_q[op, b, :, part]))
            send_q[i, op, b] = jnp.concatenate(parts, axis=0).astype(BF16)

    def scatter(op, i):
        for slot in range(1, SLOTS):
            remote(
                leaving(op, i).at[owner(op, slot)], landing(op, i).at[0, slot],
                s1_send.at[op, i], s1_recv.at[op, i], device(*plane(op, slot), core),
            ).start()
        pltpu.make_async_copy(
            leaving(op, i).at[owner(op, 0)], landing(op, i).at[0, 0], own_sem.at[op, i]
        ).start()

    def spread(op, i):
        wait_for(landing(op, i).at[0, pl.ds(1, SLOTS - 1)], s1_recv.at[op, i])
        wait_for(landing(op, i).at[0, 0], own_sem.at[op, i])
        for d, step in enumerate((1, -1)):
            remote(
                landing(op, i).at[0], landing(op, i).at[step % RING],
                s2_send.at[op, i, d], s2_recv.at[op, i, d], along(op, step),
            ).start()

    def forward(op, i):
        for d, step in enumerate((1, -1)):
            part = pl.ds(d * (SLOTS // 2), SLOTS // 2)
            wait_for(landing(op, i).at[step % RING], s2_recv.at[op, i, d])
            remote(
                landing(op, i).at[step % RING, part], landing(op, i).at[2, part],
                s3_send.at[op, i, d], s3_recv.at[op, i, d], along(op, step),
            ).start()

    def arrived(op, i):
        for d in range(2):
            part = pl.ds(d * (SLOTS // 2), SLOTS // 2)
            wait_for(landing(op, i).at[2, part], s3_recv.at[op, i, d])

    terms = subs * per_block

    def make_pick():
        row = lax.broadcasted_iota(jnp.int32, (256, 128), 0)
        for i in range(chunks):
            for h in range(2):
                for sub in range(subs):
                    lane = sub * per_block + 2 * i + h
                    one = (row == lane) | (row == terms + lane) | (row == 128 + lane)
                    at = (h * subs + sub) * 128
                    pick[i, :, at : at + 128] = jnp.where(one, 1.0, 0.0).astype(BF16)

    def split_scales(op):
        lane = lax.broadcasted_iota(jnp.int32, (RING * SLOTS * 8, 128), 1)
        s = jnp.where(lane < terms, raw_s[op].reshape(RING * SLOTS * 8, 128), 0.0)
        high = s.astype(BF16).astype(F32)
        middle = (s - high).astype(BF16).astype(F32)
        low = (s - high) - middle
        split_s[op, :, :128] = (high + pltpu.roll(middle, terms, 1)).astype(BF16)
        split_s[op, :, 128:] = low.astype(BF16)

    def standardize(op, i):
        for n in range(0, wide_s.shape[1], 256):
            wide_s[:, n : n + 256] = jnp.dot(
                split_s[op], pick[i, :, n : n + 256], preferred_element_type=F32
            )

        def add(p, carry):
            sums, squares = list(carry[0]), list(carry[1])
            at = p if op == BASE else (p % RING) * RING + p // RING
            s = wide_s[pl.ds(pl.multiple_of(p * RING * 8, RING * 8), RING * 8), :]
            parts = [[], []]
            for q in range(RING):
                block = raw[i, op, p // RING, (p % RING) * RING + q].astype(F32)
                for h in range(2):
                    for sub in range(subs):
                        n = h * subs + sub
                        parts[h].append(
                            block[n * 8 : n * 8 + 8]
                            * s[q * 8 : q * 8 + 8, n * 128 : n * 128 + 128]
                        )
            start = pl.multiple_of(at * token_ring, token_ring)
            for h in range(2):
                work[pl.ds(start, token_ring), h * HALF : (h + 1) * HALF] = jnp.concatenate(
                    parts[h], axis=0
                )
                v = parts[h]
                w = [u * u for u in v]
                while len(v) > 1:
                    v = [sum(v[j : j + 2][1:], v[j]) for j in range(0, len(v), 2)]
                    w = [sum(w[j : j + 2][1:], w[j]) for j in range(0, len(w), 2)]
                sums[h] = sums[h] + v[0]
                squares[h] = squares[h] + w[0]
            return tuple(sums), tuple(squares)

        zero = jnp.zeros((8, HALF), F32)
        sums, squares = lax.fori_loop(
            0, RING * RING, add, ((zero, zero), (zero, zero)), unroll=2
        )
        average, factor = [], []
        for h in range(2):
            a = jnp.sum(sums[h], axis=0, keepdims=True) / tokens
            spread_ = jnp.sum(squares[h], axis=0, keepdims=True) / tokens - a * a
            average.append(a)
            factor.append(lax.rsqrt(spread_ + 1e-06) * (1.0 / math.sqrt(tokens)))

        rows = 128 if op == BASE else 96

        @pl.loop(0, tokens // rows, unroll=2)
        def _(t):
            part = pl.ds(pl.multiple_of(t * rows, rows), rows)
            for h in range(2):
                u = (work[part, h * HALF : (h + 1) * HALF] - average[h]) * factor[h]
                column = slice(i * CHUNK + h * HALF, i * CHUNK + (h + 1) * HALF)
                if op == BASE:
                    base_t[column, part] = u.astype(BF16).T
                else:
                    adj_u[core, part, column] = u.astype(BF16)

    def finish(i):
        column = pl.ds(i * CHUNK, CHUNK)
        arrived(ADJ, i)
        standardize(ADJ, i)
        remote(
            adj_u.at[core, :, column], adj_u.at[core, :, column],
            swap_send.at[i], swap_recv.at[i], peer,
        ).start()
        arrived(BASE, i)
        standardize(BASE, i)
        wait_for(adj_u.at[other, :, column], swap_recv.at[i])
        if i < chunks - 1:
            multiply(base_t, adj_u, early, early, i)

    for step in range(chunks + 3):
        if step < chunks:
            for op in (BASE, ADJ):
                pack(op, step)
                scatter(op, step)
        if step == 0:
            for op in (BASE, ADJ):
                pack_scales(op)
                scatter(op, chunks)
            make_pick()
        i = step - 1
        if 0 <= i < chunks:
            for op in (BASE, ADJ):
                if i == 0:
                    spread(op, chunks)
                spread(op, i)
        i = step - 2
        if 0 <= i < chunks:
            for op in (BASE, ADJ):
                if i == 0:
                    forward(op, chunks)
                forward(op, i)
        i = step - 3
        if 0 <= i < chunks:
            if i == 0:
                for op in (BASE, ADJ):
                    arrived(op, chunks)
                    split_scales(op)
            finish(i)

    for op in (BASE, ADJ):
        wait_for(peer_q.at[op], s0_send.at[op])
        wait_for(peer_s.at[op], s0_send.at[2 + op])
        for i in range(chunks + 1):
            wait_for(landing(op, i).at[0, pl.ds(1, SLOTS - 1)], s1_send.at[op, i])
            for d in range(2):
                wait_for(landing(op, i).at[0], s2_send.at[op, i, d])
                wait_for(landing(op, i).at[0, pl.ds(0, SLOTS // 2)], s3_send.at[op, i, d])
    for i in range(chunks):
        wait_for(adj_u.at[core, :, pl.ds(i * CHUNK, CHUNK)], swap_send.at[i])


def gather(base_q, base_s, adj_q, adj_s):
    local, latents = base_q.shape
    width = latents // (OWNERS * CORES)
    chunks = width // CHUNK
    early = width - CHUNK
    tokens = local * CORES * RING**3
    rows = 2 * CORES * local
    subs = CORES * local // 8
    dma = pltpu.SemaphoreType.DMA
    whole = pl.BlockSpec(memory_space=VMEM)
    return pl.pallas_call(
        functools.partial(gather_kernel, local, width),
        out_shape=(
            VMEM((width, tokens), BF16),
            VMEM((CORES, tokens, width), BF16),
            VMEM((CORES, early, early), BF16),
        ),
        in_specs=[pl.BlockSpec(memory_space=pltpu.HBM)] * 4,
        out_specs=(whole,) * 3,
        scratch_shapes=[
            VMEM((2, OWNERS, local, width), BF16),
            VMEM((2,) + base_s.shape, F32),
            VMEM((2, OWNERS, local, width), BF16),
            VMEM((2,) + base_s.shape, F32),
            VMEM((chunks, 2, OWNERS, rows, HALF), BF16),
            VMEM((2, OWNERS, 8, 128), F32),
            VMEM((chunks, 2, RING, SLOTS, rows, HALF), BF16),
            VMEM((2, RING, SLOTS, 8, 128), F32),
            VMEM((2, RING * SLOTS * 8, 256), BF16),
            VMEM((chunks, 256, 2 * subs * 128), BF16),
            VMEM((RING * SLOTS * 8, 2 * subs * 128), F32),
            VMEM((tokens, CHUNK), F32),
            dma((2, OWNERS + 1)),
            dma((4,)), dma((4,)),
            dma((2, chunks + 1)), dma((2, chunks + 1)),
            dma((2, chunks + 1, 2)), dma((2, chunks + 1, 2)),
            dma((2, chunks + 1, 2)), dma((2, chunks + 1, 2)),
            dma((2, chunks + 1)),
            dma((chunks,)), dma((chunks,)),
        ],
        compiler_params=pltpu.CompilerParams(
            collective_id=0, has_side_effects=True, vmem_limit_bytes=27 << 20
        ),
        name="gather_units",
    )(base_q, base_s, adj_q, adj_s)


def product_kernel(base_t, adj_u, early, out, below, beside, early_sem, late_sem):
    width = base_t.shape[0]
    done_to = early.shape[1]
    moves = [
        pltpu.make_async_copy(
            early.at[half, a : a + CHUNK],
            out.at[a : a + CHUNK, half * width : half * width + done_to],
            early_sem.at[half, a // CHUNK],
        )
        for half in range(CORES)
        for a in range(0, done_to, CHUNK)
    ]
    for move in moves:
        move.start()

    def late(half, which):
        start = pl.multiple_of(half * width, width)
        if which == 0:
            at = out.at[:, pl.ds(start + done_to, CHUNK)]
            return pltpu.make_async_copy(below.at[half], at, late_sem.at[half, 0])
        at = out.at[pl.ds(done_to, CHUNK), pl.ds(start, done_to)]
        return pltpu.make_async_copy(beside.at[half], at, late_sem.at[half, 1])

    multiply(
        base_t, adj_u, below, beside, done_to // CHUNK,
        lambda half, which: late(half, which).start(),
    )
    for half in range(CORES):
        for which in range(2):
            late(half, which).wait()
    for move in moves:
        move.wait()


def product(base_t, adj_u, early):
    width = base_t.shape[0]
    whole = pl.BlockSpec(memory_space=VMEM)
    return pl.pallas_call(
        product_kernel,
        out_shape=jax.ShapeDtypeStruct((width, CORES * width), BF16),
        in_specs=[whole] * 3,
        out_specs=pl.BlockSpec(memory_space=pl.ANY),
        scratch_shapes=[
            VMEM((CORES, width, CHUNK), BF16),
            VMEM((CORES, CHUNK, width - CHUNK), BF16),
            pltpu.SemaphoreType.DMA((CORES, width // CHUNK - 1)),
            pltpu.SemaphoreType.DMA((CORES, 2)),
        ],
        compiler_params=pltpu.CompilerParams(vmem_limit_bytes=8 << 20),
        name="correlate",
    )(base_t, adj_u, early)


def on_device(*args):
    units = gather(*args)
    return product(*(pltpu.with_memory_space_constraint(u, VMEM) for u in units))


def solution(mesh):
    spec = P(("row", "col"), None)
    return jax.shard_map(
        on_device, mesh=mesh, in_specs=(spec,) * 4, out_specs=P("row", "col"), check_vma=False
    )
```

```python
import functools
import math

import jax
import jax.numpy as jnp
from jax import lax
from jax.experimental import pallas as pl
from jax.experimental.pallas import tpu as pltpu
from jax.sharding import PartitionSpec as P

MESH = pl.DeviceIdType.MESH
VMEM = pltpu.VMEM
BF16 = jnp.bfloat16
F32 = jnp.float32

CORES = 2
RING = 4
GROUP = 128
OWNERS = 8
CHIPS = RING * 2 * OWNERS
BASE, ADJ = 0, 1
CHUNK = 256
HALF = CHUNK // 2


def place():
    row, col = lax.axis_index("row"), lax.axis_index("col")
    x, z_hi = col // 2, col % 2
    y, z_lo, core = row // 4, (row // 2) % 2, row % 2
    return x, y, z_hi * 2 + z_lo, core


def device(x, y, z, core):
    x, y, z = x % RING, y % RING, z % RING
    return (y * 2 + z % 2) * CORES + core, x * 2 + z // 2


def pieces(n, most):
    count = max(1, -(-n // most))
    edges = [n // CHUNK * j // count * CHUNK for j in range(count + 1)]
    return [(a, b - a) for a, b in zip(edges, edges[1:]) if b > a]


def multiply(base_t, adj_u, below, beside, i, done=None):
    last = done is not None
    new = slice(i * CHUNK, (i + 1) * CHUNK)
    into = slice(0, CHUNK) if last else new

    @pl.loop(0, CORES)
    def _(half):
        for a, n in pieces((i + 1) * CHUNK, 1024):
            below[half, a : a + n, into] = jnp.dot(
                base_t[a : a + n, :], adj_u[half, :, new], preferred_element_type=F32
            ).astype(BF16)
        if last:
            done(half, 0)
        for a, n in pieces(i * CHUNK, 1024):
            beside[half, into, a : a + n] = jnp.dot(
                base_t[new, :], adj_u[half, :, a : a + n], preferred_element_type=F32
            ).astype(BF16)
        if last:
            done(half, 1)


def gather_kernel(
    local, width,
    base_q, base_s, adj_q, adj_s,
    base_t, adj_u, early,
    own_q, own_s, peer_q, peer_s, send_q, send_s, raw, raw_s,
    split_s, pick, wide_s, work,
    load_sem, s0_send, s0_recv, s1_send, s1_recv, ex_send, ex_recv, s2_send, s2_recv, s3_send, s3_recv,
    own_sem, swap_send, swap_recv,
):
    x, y, z, core = place()
    other = 1 - core
    chunks = width // CHUNK
    tokens = adj_u.shape[1]
    local_pair = CORES * local
    queue = (base_q, adj_q)
    scale = (base_s, adj_s)
    peer = device(x, y, z, other)

    near, far = z + 1 - 2 * (z % 2), z + 2

    def group(op, slot):
        step, across = slot // 2, slot % 2
        if op == BASE:
            return x, y + step, (near if across else z)
        return x + step, y, (far if across else z)

    def owner(op, slot):
        px, py, pz = group(op, slot)
        if op == BASE:
            return (py % RING) * 2 + pz % 2
        return (px % RING) * 2 + (pz % RING) // 2

    partner = (device(x, y, far, core), device(x, y, near, core))

    def along(op, step):
        return device(x + step, y, z, core) if op == BASE else device(x, y + step, z, core)

    def landing(op, i):
        return raw_s.at[op] if i == chunks else raw.at[i, op]

    def leaving(op, i):
        return send_s.at[op] if i == chunks else send_q.at[i, op]

    def remote(src, dst, send_sem, recv_sem, where):
        return pltpu.make_async_remote_copy(
            src_ref=src, dst_ref=dst, send_sem=send_sem, recv_sem=recv_sem,
            device_id=where, device_id_type=MESH,
        )

    def wait_for(ref, sem):
        pltpu.make_async_copy(ref, ref, sem).wait()

    loads = []
    for op in (BASE, ADJ):
        for b in range(OWNERS):
            start = pl.multiple_of((2 * b + core) * width, width)
            loads.append(
                pltpu.make_async_copy(
                    queue[op].at[:, pl.ds(start, width)], own_q.at[op, b], load_sem.at[op, b]
                )
            )
        loads.append(pltpu.make_async_copy(scale[op], own_s.at[op], load_sem.at[op, OWNERS]))
    for load in loads:
        load.start()

    barrier = pltpu.get_barrier_semaphore()
    greeted = [peer]
    for slot in range(1, OWNERS):
        greeted += [device(*group(op, slot), core) for op in (BASE, ADJ)]
    for where in greeted:
        pl.semaphore_signal(barrier, inc=1, device_id=where, device_id_type=MESH)
    pl.semaphore_wait(barrier, len(greeted))

    for op in (BASE, ADJ):
        for b in range(OWNERS):
            start = pl.multiple_of((2 * b + other) * width, width)
            remote(
                queue[op].at[:, pl.ds(start, width)], peer_q.at[op, b],
                s0_send.at[op], s0_recv.at[op], peer,
            ).start()
        remote(scale[op], peer_s.at[op], s0_send.at[2 + op], s0_recv.at[2 + op], peer).start()
    for load in loads:
        load.wait()
    for op in (BASE, ADJ):
        wait_for(peer_q.at[op], s0_recv.at[op])
        wait_for(peer_s.at[op], s0_recv.at[2 + op])

    def both_cores(own, theirs):
        own, theirs = own.astype(F32), theirs.astype(F32)
        first = jnp.where(core == 0, own, theirs)
        second = jnp.where(core == 0, theirs, own)
        return jnp.concatenate([first, second], axis=0)

    lanes = lax.broadcasted_iota(jnp.int32, (8, 128), 1)
    per_block = width // GROUP
    subs = CORES * local // 8

    def pack_scales(op):
        all_s = both_cores(own_s[op], peer_s[op])
        for b in range(OWNERS):
            tile = 2 * b * per_block // 128
            first = (2 * b * per_block) % 128
            packed = jnp.zeros((8, 128), F32)
            for sub in range(subs):
                part = all_s[sub * 8 : sub * 8 + 8, tile * 128 : tile * 128 + 128]
                shift = (sub * per_block + 256 - first - core * per_block) % 128
                part = pltpu.roll(part, shift, 1)
                mine = (lanes >= sub * per_block) & (lanes < (sub + 1) * per_block)
                packed = jnp.where(mine, part, packed)
            send_s[op, b] = packed

    def pack(op, i):
        @pl.loop(0, OWNERS)
        def _(b):
            parts = []
            for h in range(2):
                part = pl.ds(i * CHUNK + h * HALF, HALF)
                parts.append(both_cores(own_q[op, b, :, part], peer_q[op, b, :, part]))
            send_q[i, op, b] = jnp.concatenate(parts, axis=0).astype(BF16)

    def scatter(op, i):
        for slot in range(1, OWNERS):
            remote(
                leaving(op, i).at[owner(op, slot)], landing(op, i).at[0, 0, slot],
                s1_send.at[op, i], s1_recv.at[op, i], device(*group(op, slot), core),
            ).start()
        pltpu.make_async_copy(
            leaving(op, i).at[owner(op, 0)], landing(op, i).at[0, 0, 0], own_sem.at[op, i]
        ).start()

    def exchange(op, i):
        wait_for(landing(op, i).at[0, 0, pl.ds(1, OWNERS - 1)], s1_recv.at[op, i])
        wait_for(landing(op, i).at[0, 0, 0], own_sem.at[op, i])
        remote(
            landing(op, i).at[0, 0], landing(op, i).at[0, 1],
            ex_send.at[op, i], ex_recv.at[op, i], partner[op],
        ).start()

    def spread(op, i):
        wait_for(landing(op, i).at[0, 1], ex_recv.at[op, i])
        for d, step in enumerate((1, -1)):
            remote(
                landing(op, i).at[0], landing(op, i).at[step % RING],
                s2_send.at[op, i, d], s2_recv.at[op, i, d], along(op, step),
            ).start()

    def forward(op, i):
        for d, step in enumerate((1, -1)):
            wait_for(landing(op, i).at[step % RING], s2_recv.at[op, i, d])
            remote(
                landing(op, i).at[step % RING, d], landing(op, i).at[2, d],
                s3_send.at[op, i, d], s3_recv.at[op, i, d], along(op, step),
            ).start()

    def arrived(op, i):
        for d in range(2):
            wait_for(landing(op, i).at[2, d], s3_recv.at[op, i, d])

    terms = subs * per_block

    def make_pick():
        row = lax.broadcasted_iota(jnp.int32, (256, 128), 0)
        for i in range(chunks):
            for h in range(2):
                for sub in range(subs):
                    lane = sub * per_block + 2 * i + h
                    one = (row == lane) | (row == terms + lane) | (row == 128 + lane)
                    at = (h * subs + sub) * 128
                    pick[i, :, at : at + 128] = jnp.where(one, 1.0, 0.0).astype(BF16)

    def split_scales(op):
        lane = lax.broadcasted_iota(jnp.int32, (CHIPS * 8, 128), 1)
        s = jnp.where(lane < terms, raw_s[op].reshape(CHIPS * 8, 128), 0.0)
        high = s.astype(BF16).astype(F32)
        middle = (s - high).astype(BF16).astype(F32)
        low = (s - high) - middle
        split_s[op, :, :128] = (high + pltpu.roll(middle, terms, 1)).astype(BF16)
        split_s[op, :, 128:] = low.astype(BF16)

    def standardize(op, i):
        for n in range(0, wide_s.shape[1], 256):
            wide_s[:, n : n + 256] = jnp.dot(
                split_s[op], pick[i, :, n : n + 256], preferred_element_type=F32
            )

        def add(p, carry):
            sums, squares = list(carry[0]), list(carry[1])
            s = wide_s[pl.ds(pl.multiple_of(p * 32, 32), 32), :]
            parts = [[], []]
            for q in range(4):
                block = raw[i, op, p // 4, (p // 2) % 2, (p % 2) * 4 + q].astype(F32)
                at = p * 4 + q
                if op == ADJ:
                    at = (p % 2) * 32 + (q // 2) * 16 + (q % 2) * 8 + p // 2
                part = pl.ds(pl.multiple_of(at * local_pair, 8), local_pair)
                for h in range(2):
                    mine = [
                        block[n * 8 : n * 8 + 8] * s[q * 8 : q * 8 + 8, n * 128 : n * 128 + 128]
                        for n in range(h * subs, (h + 1) * subs)
                    ]
                    work[part, h * HALF : (h + 1) * HALF] = jnp.concatenate(mine, axis=0)
                    parts[h] += mine
            for h in range(2):
                v = parts[h]
                w = [u * u for u in v]
                while len(v) > 1:
                    v = [sum(v[j : j + 2][1:], v[j]) for j in range(0, len(v), 2)]
                    w = [sum(w[j : j + 2][1:], w[j]) for j in range(0, len(w), 2)]
                sums[h] = sums[h] + v[0]
                squares[h] = squares[h] + w[0]
            return tuple(sums), tuple(squares)

        zero = jnp.zeros((8, HALF), F32)
        sums, squares = lax.fori_loop(
            0, CHIPS // 4, add, ((zero, zero), (zero, zero)), unroll=2
        )
        average, factor = [], []
        for h in range(2):
            a = jnp.sum(sums[h], axis=0, keepdims=True) / tokens
            spread_ = jnp.sum(squares[h], axis=0, keepdims=True) / tokens - a * a
            average.append(a)
            factor.append(lax.rsqrt(spread_ + 1e-06) * (1.0 / math.sqrt(tokens)))

        rows = 128 if op == BASE else 96

        @pl.loop(0, tokens // rows, unroll=2)
        def _(t):
            part = pl.ds(pl.multiple_of(t * rows, rows), rows)
            for h in range(2):
                u = (work[part, h * HALF : (h + 1) * HALF] - average[h]) * factor[h]
                column = slice(i * CHUNK + h * HALF, i * CHUNK + (h + 1) * HALF)
                if op == BASE:
                    base_t[column, part] = u.astype(BF16).T
                else:
                    adj_u[core, part, column] = u.astype(BF16)

    def finish(i):
        column = pl.ds(i * CHUNK, CHUNK)
        arrived(ADJ, i)
        standardize(ADJ, i)
        remote(
            adj_u.at[core, :, column], adj_u.at[core, :, column],
            swap_send.at[i], swap_recv.at[i], peer,
        ).start()
        arrived(BASE, i)
        standardize(BASE, i)

    def both(do, i):
        if 0 <= i < chunks:
            for op in (BASE, ADJ):
                do(op, i)

    def depart(op, i):
        pack(op, i)
        scatter(op, i)

    both(depart, 0)
    for op in (BASE, ADJ):
        pack_scales(op)
        scatter(op, chunks)
    both(depart, 1)
    both(exchange, 0)
    for op in (BASE, ADJ):
        exchange(op, chunks)
    both(depart, 2)
    both(spread, 0)
    for op in (BASE, ADJ):
        spread(op, chunks)
    both(exchange, 1)
    both(depart, 3)
    make_pick()
    both(spread, 1)
    both(exchange, 2)
    for i in range(chunks + 1):
        both(forward, i)
        if i == 0:
            for op in (BASE, ADJ):
                forward(op, chunks)
        if i == 1:
            for op in (BASE, ADJ):
                arrived(op, chunks)
                split_scales(op)
        if i:
            finish(i - 1)
        both(spread, i + 2)
        both(exchange, i + 3)
        both(depart, i + 4)
        if i:
            wait_for(adj_u.at[other, :, pl.ds((i - 1) * CHUNK, CHUNK)], swap_recv.at[i - 1])
            if i < chunks:
                multiply(base_t, adj_u, early, early, i - 1)

    for op in (BASE, ADJ):
        wait_for(peer_q.at[op], s0_send.at[op])
        wait_for(peer_s.at[op], s0_send.at[2 + op])
        for i in range(chunks + 1):
            wait_for(landing(op, i).at[0, 0, pl.ds(1, OWNERS - 1)], s1_send.at[op, i])
            wait_for(landing(op, i).at[0, 0], ex_send.at[op, i])
            for d in range(2):
                wait_for(landing(op, i).at[0], s2_send.at[op, i, d])
                wait_for(landing(op, i).at[0, 0], s3_send.at[op, i, d])
    for i in range(chunks):
        wait_for(adj_u.at[core, :, pl.ds(i * CHUNK, CHUNK)], swap_send.at[i])


def gather(base_q, base_s, adj_q, adj_s):
    local, latents = base_q.shape
    width = latents // (OWNERS * CORES)
    chunks = width // CHUNK
    early = width - CHUNK
    tokens = local * CORES * RING**3
    rows = 2 * CORES * local
    subs = CORES * local // 8
    dma = pltpu.SemaphoreType.DMA
    whole = pl.BlockSpec(memory_space=VMEM)
    return pl.pallas_call(
        functools.partial(gather_kernel, local, width),
        out_shape=(
            VMEM((width, tokens), BF16),
            VMEM((CORES, tokens, width), BF16),
            VMEM((CORES, early, early), BF16),
        ),
        in_specs=[pl.BlockSpec(memory_space=pltpu.HBM)] * 4,
        out_specs=(whole,) * 3,
        scratch_shapes=[
            VMEM((2, OWNERS, local, width), BF16),
            VMEM((2,) + base_s.shape, F32),
            VMEM((2, OWNERS, local, width), BF16),
            VMEM((2,) + base_s.shape, F32),
            VMEM((chunks, 2, OWNERS, rows, HALF), BF16),
            VMEM((2, OWNERS, 8, 128), F32),
            VMEM((chunks, 2, RING, 2, OWNERS, rows, HALF), BF16),
            VMEM((2, RING, 2, OWNERS, 8, 128), F32),
            VMEM((2, CHIPS * 8, 256), BF16),
            VMEM((chunks, 256, 2 * subs * 128), BF16),
            VMEM((CHIPS * 8, 2 * subs * 128), F32),
            VMEM((tokens, CHUNK), F32),
            dma((2, OWNERS + 1)),
            dma((4,)), dma((4,)),
            dma((2, chunks + 1)), dma((2, chunks + 1)),
            dma((2, chunks + 1)), dma((2, chunks + 1)),
            dma((2, chunks + 1, 2)), dma((2, chunks + 1, 2)),
            dma((2, chunks + 1, 2)), dma((2, chunks + 1, 2)),
            dma((2, chunks + 1)),
            dma((chunks,)), dma((chunks,)),
        ],
        compiler_params=pltpu.CompilerParams(
            collective_id=0, has_side_effects=True, vmem_limit_bytes=27 << 20
        ),
        name="gather_units",
    )(base_q, base_s, adj_q, adj_s)


def product_kernel(base_t, adj_u, early, out, below, beside, early_sem, late_sem):
    width = base_t.shape[0]
    done_to = early.shape[1]
    moves = [
        pltpu.make_async_copy(
            early.at[half, a : a + CHUNK],
            out.at[a : a + CHUNK, half * width : half * width + done_to],
            early_sem.at[half, a // CHUNK],
        )
        for half in range(CORES)
        for a in range(0, done_to, CHUNK)
    ]
    for move in moves:
        move.start()

    def late(half, which):
        start = pl.multiple_of(half * width, width)
        if which == 0:
            at = out.at[:, pl.ds(start + done_to, CHUNK)]
            return pltpu.make_async_copy(below.at[half], at, late_sem.at[half, 0])
        at = out.at[pl.ds(done_to, CHUNK), pl.ds(start, done_to)]
        return pltpu.make_async_copy(beside.at[half], at, late_sem.at[half, 1])

    multiply(
        base_t, adj_u, below, beside, done_to // CHUNK,
        lambda half, which: late(half, which).start(),
    )
    for half in range(CORES):
        for which in range(2):
            late(half, which).wait()
    for move in moves:
        move.wait()


def product(base_t, adj_u, early):
    width = base_t.shape[0]
    whole = pl.BlockSpec(memory_space=VMEM)
    return pl.pallas_call(
        product_kernel,
        out_shape=jax.ShapeDtypeStruct((width, CORES * width), BF16),
        in_specs=[whole] * 3,
        out_specs=pl.BlockSpec(memory_space=pl.ANY),
        scratch_shapes=[
            VMEM((CORES, width, CHUNK), BF16),
            VMEM((CORES, CHUNK, width - CHUNK), BF16),
            pltpu.SemaphoreType.DMA((CORES, width // CHUNK - 1)),
            pltpu.SemaphoreType.DMA((CORES, 2)),
        ],
        compiler_params=pltpu.CompilerParams(vmem_limit_bytes=8 << 20),
        name="correlate",
    )(base_t, adj_u, early)


def on_device(*args):
    units = gather(*args)
    return product(*(pltpu.with_memory_space_constraint(u, VMEM) for u in units))


def solution(mesh):
    spec = P(("row", "col"), None)
    return jax.shard_map(
        on_device, mesh=mesh, in_specs=(spec,) * 4, out_specs=P("row", "col"), check_vma=False
    )
```

```python
import functools
import math

import jax
import jax.numpy as jnp
from jax import lax
from jax.experimental import pallas as pl
from jax.experimental.pallas import tpu as pltpu
from jax.sharding import PartitionSpec as P

MESH = pl.DeviceIdType.MESH
VMEM = pltpu.VMEM
BF16 = jnp.bfloat16
F32 = jnp.float32

CORES = 2
RING = 4
GROUP = 128
OWNERS = 8
CHIPS = RING * 2 * OWNERS
BASE, ADJ = 0, 1
CHUNK = 256
HALF = CHUNK // 2


ORDER = (
    "d0A d8A d1B d8B",
    "d0B d1A d3B d2A",
    "pick e0A e8A e0B",
    "e8B e1A e1B d7B",
    "d2B d3A e2A d6B",
    "d4A s0A s8A s0B",
    "s8B s1A s1B e2B",
    "f0A f8A e3A e3B",
    "d4B f0B f8B d6A",
    "s2A d5A e4A d5B",
    "f1A f1B s2B t8B",
    "t0B s3A s3B f2A",
    "e4B t8A t0A e5A",
    "d7A s4A f2B t1B",
    "e5B e6A e6B t1A",
    "s4B f3A t2A m0a",
    "f3B s5A m1a t2B",
    "m2b s5B f4A e7A",
    "e7B m1b t3A s6A",
    "f4B m2a t3B s6B",
    "f5A m3a s7A t4A",
    "m3b f5B s7B t4B",
    "f6A m4a t5A f6B",
    "m4b t5B f7A m5a",
    "t6A f7B m5b t6B",
    "m6b t7A m6a t7B",
    "m0b",
)


def place():
    row, col = lax.axis_index("row"), lax.axis_index("col")
    x, z_hi = col // 2, col % 2
    y, z_lo, core = row // 4, (row // 2) % 2, row % 2
    return x, y, z_hi * 2 + z_lo, core


def device(x, y, z, core):
    x, y, z = x % RING, y % RING, z % RING
    return (y * 2 + z % 2) * CORES + core, x * 2 + z // 2


def pieces(n, most):
    count = max(1, -(-n // most))
    edges = [n // CHUNK * j // count * CHUNK for j in range(count + 1)]
    return [(a, b - a) for a, b in zip(edges, edges[1:]) if b > a]


def columns(base_t, adj_u, out, i, at, half):
    new = slice(i * CHUNK, (i + 1) * CHUNK)
    for a, n in pieces((i + 1) * CHUNK, 1024):
        out[half, a : a + n, at : at + CHUNK] = jnp.dot(
            base_t[a : a + n, :], adj_u[half, :, new], preferred_element_type=F32
        ).astype(BF16)


def rows(base_t, adj_u, out, i, at, half):
    new = slice(i * CHUNK, (i + 1) * CHUNK)
    for a, n in pieces(i * CHUNK, 1024):
        out[half, at : at + CHUNK, a : a + n] = jnp.dot(
            base_t[new, :], adj_u[half, :, a : a + n], preferred_element_type=F32
        ).astype(BF16)


def gather_kernel(
    local, width,
    base_q, base_s, adj_q, adj_s,
    base_t, adj_u, early,
    own_q, own_s, peer_q, peer_s, send_q, send_s, raw, raw_s,
    split_s, pick, wide_s, work,
    load_sem, s0_send, s0_recv, s1_send, s1_recv, ex_send, ex_recv, s2_send, s2_recv, s3_send, s3_recv,
    own_sem, swap_send, swap_recv,
):
    x, y, z, core = place()
    other = 1 - core
    chunks = width // CHUNK
    tokens = adj_u.shape[1]
    local_pair = CORES * local
    queue = (base_q, adj_q)
    scale = (base_s, adj_s)
    peer = device(x, y, z, other)

    near, far = z + 1 - 2 * (z % 2), z + 2

    def group(op, slot):
        step, across = slot // 2, slot % 2
        if op == BASE:
            return x, y + step, (near if across else z)
        return x + step, y, (far if across else z)

    def owner(op, slot):
        px, py, pz = group(op, slot)
        if op == BASE:
            return (py % RING) * 2 + pz % 2
        return (px % RING) * 2 + (pz % RING) // 2

    partner = (device(x, y, far, core), device(x, y, near, core))

    def along(op, step):
        return device(x + step, y, z, core) if op == BASE else device(x, y + step, z, core)

    def landing(op, i):
        return raw_s.at[op] if i == chunks else raw.at[i, op]

    def leaving(op, i):
        return send_s.at[op] if i == chunks else send_q.at[i, op]

    def remote(src, dst, send_sem, recv_sem, where):
        return pltpu.make_async_remote_copy(
            src_ref=src, dst_ref=dst, send_sem=send_sem, recv_sem=recv_sem,
            device_id=where, device_id_type=MESH,
        )

    def wait_for(ref, sem):
        pltpu.make_async_copy(ref, ref, sem).wait()

    loads = []
    for op in (BASE, ADJ):
        for b in range(OWNERS):
            start = pl.multiple_of((2 * b + core) * width, width)
            loads.append(
                pltpu.make_async_copy(
                    queue[op].at[:, pl.ds(start, width)], own_q.at[op, b], load_sem.at[op, b]
                )
            )
        loads.append(pltpu.make_async_copy(scale[op], own_s.at[op], load_sem.at[op, OWNERS]))
    for load in loads:
        load.start()

    barrier = pltpu.get_barrier_semaphore()
    greeted = [peer]
    for slot in range(1, OWNERS):
        greeted += [device(*group(op, slot), core) for op in (BASE, ADJ)]
    for where in greeted:
        pl.semaphore_signal(barrier, inc=1, device_id=where, device_id_type=MESH)
    pl.semaphore_wait(barrier, len(greeted))

    for op in (BASE, ADJ):
        for b in range(OWNERS):
            start = pl.multiple_of((2 * b + other) * width, width)
            remote(
                queue[op].at[:, pl.ds(start, width)], peer_q.at[op, b],
                s0_send.at[op], s0_recv.at[op], peer,
            ).start()
        remote(scale[op], peer_s.at[op], s0_send.at[2 + op], s0_recv.at[2 + op], peer).start()
    for load in loads:
        load.wait()
    for op in (BASE, ADJ):
        wait_for(peer_q.at[op], s0_recv.at[op])
        wait_for(peer_s.at[op], s0_recv.at[2 + op])

    def both_cores(own, theirs):
        own, theirs = own.astype(F32), theirs.astype(F32)
        first = jnp.where(core == 0, own, theirs)
        second = jnp.where(core == 0, theirs, own)
        return jnp.concatenate([first, second], axis=0)

    lanes = lax.broadcasted_iota(jnp.int32, (8, 128), 1)
    per_block = width // GROUP
    subs = CORES * local // 8

    def pack_scales(op):
        all_s = both_cores(own_s[op], peer_s[op])
        for b in range(OWNERS):
            tile = 2 * b * per_block // 128
            first = (2 * b * per_block) % 128
            packed = jnp.zeros((8, 128), F32)
            for sub in range(subs):
                part = all_s[sub * 8 : sub * 8 + 8, tile * 128 : tile * 128 + 128]
                shift = (sub * per_block + 256 - first - core * per_block) % 128
                part = pltpu.roll(part, shift, 1)
                mine = (lanes >= sub * per_block) & (lanes < (sub + 1) * per_block)
                packed = jnp.where(mine, part, packed)
            send_s[op, b] = packed

    def pack(op, i):
        @pl.loop(0, OWNERS)
        def _(b):
            parts = []
            for h in range(2):
                part = pl.ds(i * CHUNK + h * HALF, HALF)
                parts.append(both_cores(own_q[op, b, :, part], peer_q[op, b, :, part]))
            send_q[i, op, b] = jnp.concatenate(parts, axis=0).astype(BF16)

    def scatter(op, i):
        for slot in range(1, OWNERS):
            remote(
                leaving(op, i).at[owner(op, slot)], landing(op, i).at[0, 0, slot],
                s1_send.at[op, i], s1_recv.at[op, i], device(*group(op, slot), core),
            ).start()
        pltpu.make_async_copy(
            leaving(op, i).at[owner(op, 0)], landing(op, i).at[0, 0, 0], own_sem.at[op, i]
        ).start()

    def exchange(op, i):
        wait_for(landing(op, i).at[0, 0, pl.ds(1, OWNERS - 1)], s1_recv.at[op, i])
        wait_for(landing(op, i).at[0, 0, 0], own_sem.at[op, i])
        remote(
            landing(op, i).at[0, 0], landing(op, i).at[0, 1],
            ex_send.at[op, i], ex_recv.at[op, i], partner[op],
        ).start()

    def spread(op, i):
        wait_for(landing(op, i).at[0, 1], ex_recv.at[op, i])
        for d, step in enumerate((1, -1)):
            remote(
                landing(op, i).at[0], landing(op, i).at[step % RING],
                s2_send.at[op, i, d], s2_recv.at[op, i, d], along(op, step),
            ).start()

    def forward(op, i):
        for d, step in enumerate((1, -1)):
            wait_for(landing(op, i).at[step % RING], s2_recv.at[op, i, d])
            remote(
                landing(op, i).at[step % RING, d], landing(op, i).at[2, d],
                s3_send.at[op, i, d], s3_recv.at[op, i, d], along(op, step),
            ).start()

    def arrived(op, i):
        for d in range(2):
            wait_for(landing(op, i).at[2, d], s3_recv.at[op, i, d])

    terms = subs * per_block

    def make_pick():
        row = lax.broadcasted_iota(jnp.int32, (256, 128), 0)
        for i in range(chunks):
            for h in range(2):
                for sub in range(subs):
                    lane = sub * per_block + 2 * i + h
                    one = (row == lane) | (row == terms + lane) | (row == 128 + lane)
                    at = (h * subs + sub) * 128
                    pick[i, :, at : at + 128] = jnp.where(one, 1.0, 0.0).astype(BF16)

    def split_scales(op):
        lane = lax.broadcasted_iota(jnp.int32, (CHIPS * 8, 128), 1)
        s = jnp.where(lane < terms, raw_s[op].reshape(CHIPS * 8, 128), 0.0)
        high = s.astype(BF16).astype(F32)
        middle = (s - high).astype(BF16).astype(F32)
        low = (s - high) - middle
        split_s[op, :, :128] = (high + pltpu.roll(middle, terms, 1)).astype(BF16)
        split_s[op, :, 128:] = low.astype(BF16)

    def standardize(op, i):
        for n in range(0, wide_s.shape[1], 256):
            wide_s[:, n : n + 256] = jnp.dot(
                split_s[op], pick[i, :, n : n + 256], preferred_element_type=F32
            )

        def add(p, carry):
            sums, squares = list(carry[0]), list(carry[1])
            parts = [[], []]
            for q in range(OWNERS):
                block = raw[i, op, p // 2, p % 2, q].astype(F32)
                at = p * OWNERS + q
                if op == ADJ:
                    at = (q // 2) * 16 + (q % 2) * 8 + p
                part = pl.ds(pl.multiple_of(at * local_pair, 8), local_pair)
                s = pl.ds(pl.multiple_of((p * OWNERS + q) * 8, 8), 8)
                for h in range(2):
                    mine = [
                        block[n * 8 : n * 8 + 8] * wide_s[s, n * 128 : n * 128 + 128]
                        for n in range(h * subs, (h + 1) * subs)
                    ]
                    work[part, h * HALF : (h + 1) * HALF] = jnp.concatenate(mine, axis=0)
                    parts[h] += mine
            for h in range(2):
                v = parts[h]
                w = [u * u for u in v]
                while len(v) > 1:
                    v = [sum(v[j : j + 2][1:], v[j]) for j in range(0, len(v), 2)]
                    w = [sum(w[j : j + 2][1:], w[j]) for j in range(0, len(w), 2)]
                sums[h] = sums[h] + v[0]
                squares[h] = squares[h] + w[0]
            return tuple(sums), tuple(squares)

        zero = jnp.zeros((8, HALF), F32)
        sums, squares = lax.fori_loop(
            0, CHIPS // OWNERS, add, ((zero, zero), (zero, zero)), unroll=2
        )
        average, factor = [], []
        for h in range(2):
            a = jnp.sum(sums[h], axis=0, keepdims=True) / tokens
            spread_ = jnp.sum(squares[h], axis=0, keepdims=True) / tokens - a * a
            average.append(a)
            factor.append(lax.rsqrt(spread_ + 1e-06) * (1.0 / math.sqrt(tokens)))

        rows = 128 if op == BASE else 96

        @pl.loop(0, tokens // rows, unroll=3 if op == BASE else 4)
        def _(t):
            part = pl.ds(pl.multiple_of(t * rows, rows), rows)
            for h in range(2):
                u = (work[part, h * HALF : (h + 1) * HALF] - average[h]) * factor[h]
                column = slice(i * CHUNK + h * HALF, i * CHUNK + (h + 1) * HALF)
                if op == BASE:
                    base_t[column, part] = u.astype(BF16).T
                else:
                    adj_u[core, part, column] = u.astype(BF16)

    swapped = set()

    def depart(op, i):
        if i < chunks:
            pack(op, i)
        else:
            pack_scales(op)
        scatter(op, i)

    def settle(op, i):
        arrived(op, i)
        if i == chunks:
            split_scales(op)
            return
        standardize(op, i)
        if op == ADJ:
            mine = adj_u.at[core, :, pl.ds(i * CHUNK, CHUNK)]
            remote(mine, mine, swap_send.at[i], swap_recv.at[i], peer).start()

    def multiply(part, i):
        if i not in swapped:
            swapped.add(i)
            wait_for(adj_u.at[other, :, pl.ds(i * CHUNK, CHUNK)], swap_recv.at[i])

        @pl.loop(0, CORES)
        def _(half):
            (columns, rows)[part](base_t, adj_u, early, i, i * CHUNK, half)

    stage = {
        "d": depart, "e": exchange, "s": spread, "f": forward, "t": settle, "m": multiply,
    }
    for word in " ".join(ORDER).split():
        if word == "pick":
            make_pick()
        elif word != "m0b":
            stage[word[0]]("BA".index(word[2]) if word[0] != "m" else "ab".index(word[2]), int(word[1]))
    i = chunks - 1
    wait_for(adj_u.at[other, :, pl.ds(i * CHUNK, CHUNK)], swap_recv.at[i])

    for op in (BASE, ADJ):
        wait_for(peer_q.at[op], s0_send.at[op])
        wait_for(peer_s.at[op], s0_send.at[2 + op])
        for i in range(chunks + 1):
            wait_for(landing(op, i).at[0, 0, pl.ds(1, OWNERS - 1)], s1_send.at[op, i])
            wait_for(landing(op, i).at[0, 0], ex_send.at[op, i])
            for d in range(2):
                wait_for(landing(op, i).at[0], s2_send.at[op, i, d])
                wait_for(landing(op, i).at[0, 0], s3_send.at[op, i, d])
    for i in range(chunks):
        wait_for(adj_u.at[core, :, pl.ds(i * CHUNK, CHUNK)], swap_send.at[i])


def gather(base_q, base_s, adj_q, adj_s):
    local, latents = base_q.shape
    width = latents // (OWNERS * CORES)
    chunks = width // CHUNK
    early = width - CHUNK
    tokens = local * CORES * RING**3
    rows = 2 * CORES * local
    subs = CORES * local // 8
    dma = pltpu.SemaphoreType.DMA
    whole = pl.BlockSpec(memory_space=VMEM)
    return pl.pallas_call(
        functools.partial(gather_kernel, local, width),
        out_shape=(
            VMEM((width, tokens), BF16),
            VMEM((CORES, tokens, width), BF16),
            VMEM((CORES, early, early), BF16),
        ),
        in_specs=[pl.BlockSpec(memory_space=pltpu.HBM)] * 4,
        out_specs=(whole,) * 3,
        scratch_shapes=[
            VMEM((2, OWNERS, local, width), BF16),
            VMEM((2,) + base_s.shape, F32),
            VMEM((2, OWNERS, local, width), BF16),
            VMEM((2,) + base_s.shape, F32),
            VMEM((chunks, 2, OWNERS, rows, HALF), BF16),
            VMEM((2, OWNERS, 8, 128), F32),
            VMEM((chunks, 2, RING, 2, OWNERS, rows, HALF), BF16),
            VMEM((2, RING, 2, OWNERS, 8, 128), F32),
            VMEM((2, CHIPS * 8, 256), BF16),
            VMEM((chunks, 256, 2 * subs * 128), BF16),
            VMEM((CHIPS * 8, 2 * subs * 128), F32),
            VMEM((tokens, CHUNK), F32),
            dma((2, OWNERS + 1)),
            dma((4,)), dma((4,)),
            dma((2, chunks + 1)), dma((2, chunks + 1)),
            dma((2, chunks + 1)), dma((2, chunks + 1)),
            dma((2, chunks + 1, 2)), dma((2, chunks + 1, 2)),
            dma((2, chunks + 1, 2)), dma((2, chunks + 1, 2)),
            dma((2, chunks + 1)),
            dma((chunks,)), dma((chunks,)),
        ],
        compiler_params=pltpu.CompilerParams(
            collective_id=0, has_side_effects=True, vmem_limit_bytes=27 << 20
        ),
        name="gather_units",
    )(base_q, base_s, adj_q, adj_s)


def product_kernel(base_t, adj_u, early, out, below, beside, early_sem, late_sem):
    width = base_t.shape[0]
    done_to = early.shape[1]
    moves = [
        pltpu.make_async_copy(
            early.at[half, a : a + CHUNK],
            out.at[a : a + CHUNK, half * width : half * width + done_to],
            early_sem.at[half, a // CHUNK],
        )
        for half in range(CORES)
        for a in range(0, done_to, CHUNK)
    ]
    for move in moves:
        move.start()

    def late(half, which):
        start = pl.multiple_of(half * width, width)
        if which == 0:
            at = out.at[:, pl.ds(start + done_to, CHUNK)]
            return pltpu.make_async_copy(below.at[half], at, late_sem.at[half, 0])
        at = out.at[pl.ds(done_to, CHUNK), pl.ds(start, done_to)]
        return pltpu.make_async_copy(beside.at[half], at, late_sem.at[half, 1])

    @pl.loop(0, CORES)
    def _(half):
        columns(base_t, adj_u, below, done_to // CHUNK, 0, half)
        late(half, 0).start()
        rows(base_t, adj_u, beside, done_to // CHUNK, 0, half)
        late(half, 1).start()

    for half in range(CORES):
        for which in range(2):
            late(half, which).wait()
    for move in moves:
        move.wait()


def product(base_t, adj_u, early):
    width = base_t.shape[0]
    whole = pl.BlockSpec(memory_space=VMEM)
    return pl.pallas_call(
        product_kernel,
        out_shape=jax.ShapeDtypeStruct((width, CORES * width), BF16),
        in_specs=[whole] * 3,
        out_specs=pl.BlockSpec(memory_space=pl.ANY),
        scratch_shapes=[
            VMEM((CORES, width, CHUNK), BF16),
            VMEM((CORES, CHUNK, width - CHUNK), BF16),
            pltpu.SemaphoreType.DMA((CORES, width // CHUNK - 1)),
            pltpu.SemaphoreType.DMA((CORES, 2)),
        ],
        compiler_params=pltpu.CompilerParams(vmem_limit_bytes=8 << 20),
        name="correlate",
    )(base_t, adj_u, early)


def on_device(*args):
    units = gather(*args)
    return product(*(pltpu.with_memory_space_constraint(u, VMEM) for u in units))


def solution(mesh):
    spec = P(("row", "col"), None)
    return jax.shard_map(
        on_device, mesh=mesh, in_specs=(spec,) * 4, out_specs=P("row", "col"), check_vma=False
    )
```

```python
import functools
import math

import jax
import jax.numpy as jnp
from jax import lax
from jax.experimental import pallas as pl
from jax.experimental.pallas import tpu as pltpu
from jax.sharding import PartitionSpec as P

MESH = pl.DeviceIdType.MESH
VMEM = pltpu.VMEM
BF16 = jnp.bfloat16
F32 = jnp.float32

CORES = 2
RING = 4
GROUP = 128
OWNERS = 8
CHIPS = RING * 2 * OWNERS
BASE, ADJ = 0, 1
CHUNK = 256
HALF = CHUNK // 2
DIRECT = (0, 8)


ORDER = (
    "d1A d1B d0A d0B",
    "d8A d8B e1A d2B",
    "e1B pick d4B d4A",
    "s0A s8A d2A s0B",
    "s8B s1A d3A d3B",
    "e2B s1B f0A f8A",
    "e2A d6B f0B f8B",
    "e3A d5A f1A d5B",
    "e3B e4A s2B e4B",
    "d7B f1B d6A s2A",
    "s3A d7A t8A t1A",
    "t0A f2B e5A e5B",
    "f2A s3B t8B t1B",
    "t0B s4A s4B f3A",
    "e6A m0a m1a t2A",
    "e6B f3B e7B s5A",
    "t2B s5B e7A f4A",
    "m2b t3A s6A f4B",
    "m1b t3B s6B m2a",
    "m3a f5A t4A f5B",
    "s7A m3b t4B s7B",
    "m4a f6A f6B t5A",
    "m4b t5B m5a f7A",
    "f7B m0b t6A m5b",
    "t6B m6a t7A m6b",
    "t7B",
)


def place():
    row, col = lax.axis_index("row"), lax.axis_index("col")
    x, z_hi = col // 2, col % 2
    y, z_lo, core = row // 4, (row // 2) % 2, row % 2
    return x, y, z_hi * 2 + z_lo, core


def device(x, y, z, core):
    x, y, z = x % RING, y % RING, z % RING
    return (y * 2 + z % 2) * CORES + core, x * 2 + z // 2


def pieces(n, most):
    count = max(1, -(-n // most))
    edges = [n // CHUNK * j // count * CHUNK for j in range(count + 1)]
    return [(a, b - a) for a, b in zip(edges, edges[1:]) if b > a]


def columns(base_t, adj_u, out, i, at, half):
    new = slice(i * CHUNK, (i + 1) * CHUNK)
    for a, n in pieces((i + 1) * CHUNK, 1024):
        out[half, a : a + n, at : at + CHUNK] = jnp.dot(
            base_t[a : a + n, :], adj_u[half, :, new], preferred_element_type=F32
        ).astype(BF16)


def rows(base_t, adj_u, out, i, at, half):
    new = slice(i * CHUNK, (i + 1) * CHUNK)
    for a, n in pieces(i * CHUNK, 1024):
        out[half, at : at + CHUNK, a : a + n] = jnp.dot(
            base_t[new, :], adj_u[half, :, a : a + n], preferred_element_type=F32
        ).astype(BF16)


def gather_kernel(
    local, width,
    base_q, base_s, adj_q, adj_s,
    base_t, adj_u, early,
    own_q, own_s, peer_q, peer_s, send_q, send_s, raw, first_s, raw_s,
    split_s, pick, wide_s, work,
    load_sem, s0_send, s0_recv, s1_send, s1_recv, ex_send, ex_recv, s2_send, s2_recv, s3_send, s3_recv,
    own_sem, swap_send, swap_recv,
):
    x, y, z, core = place()
    other = 1 - core
    chunks = width // CHUNK
    tokens = adj_u.shape[1]
    local_pair = CORES * local
    queue = (base_q, adj_q)
    scale = (base_s, adj_s)
    peer = device(x, y, z, other)

    near, far = z + 1 - 2 * (z % 2), z + 2

    def group(op, slot, side=0):
        step, across = slot // 2, slot % 2
        if op == BASE:
            return x, y + step, (near if across else z) + 2 * side
        return x + step, y, (far if across else z) + (near - z) * side

    def owner(op, slot):
        px, py, pz = group(op, slot)
        if op == BASE:
            return (py % RING) * 2 + pz % 2
        return (px % RING) * 2 + (pz % RING) // 2

    partner = (device(x, y, far, core), device(x, y, near, core))

    def along(op, step):
        return device(x + step, y, z, core) if op == BASE else device(x, y + step, z, core)

    def inbox(op, i):
        return first_s.at[op] if i == chunks else raw.at[i, op, 0]

    def slab(op, i, step):
        return raw_s.at[op, step % RING] if i == chunks else raw.at[i, op, step % RING]

    def half(op, i, step, d):
        if i == chunks:
            return raw_s.at[op, step % RING, pl.ds(d * (OWNERS // 2), OWNERS // 2)]
        return raw.at[i, op, step % RING, d]

    def leaving(op, i):
        return send_s.at[op] if i == chunks else send_q.at[i, op]

    def remote(src, dst, send_sem, recv_sem, where):
        return pltpu.make_async_remote_copy(
            src_ref=src, dst_ref=dst, send_sem=send_sem, recv_sem=recv_sem,
            device_id=where, device_id_type=MESH,
        )

    def wait_for(ref, sem):
        pltpu.make_async_copy(ref, ref, sem).wait()

    loads = []
    for op in (BASE, ADJ):
        for b in range(OWNERS):
            start = pl.multiple_of((2 * b + core) * width, width)
            loads.append(
                pltpu.make_async_copy(
                    queue[op].at[:, pl.ds(start, width)], own_q.at[op, b], load_sem.at[op, b]
                )
            )
        loads.append(pltpu.make_async_copy(scale[op], own_s.at[op], load_sem.at[op, OWNERS]))
    for load in loads:
        load.start()

    barrier = pltpu.get_barrier_semaphore()
    greeted = [peer]
    for slot in range(1, OWNERS):
        greeted += [device(*group(op, slot), core) for op in (BASE, ADJ)]
        greeted += [device(*group(op, slot, 1), core) for op in (BASE, ADJ)[: slot]]
    for where in greeted:
        pl.semaphore_signal(barrier, inc=1, device_id=where, device_id_type=MESH)
    pl.semaphore_wait(barrier, len(greeted))

    for op in (BASE, ADJ):
        for b in range(OWNERS):
            start = pl.multiple_of((2 * b + other) * width, width)
            remote(
                queue[op].at[:, pl.ds(start, width)], peer_q.at[op, b],
                s0_send.at[op], s0_recv.at[op], peer,
            ).start()
        remote(scale[op], peer_s.at[op], s0_send.at[2 + op], s0_recv.at[2 + op], peer).start()
    for load in loads:
        load.wait()

    def both_cores(own, theirs):
        own, theirs = own.astype(F32), theirs.astype(F32)
        first = jnp.where(core == 0, own, theirs)
        second = jnp.where(core == 0, theirs, own)
        return jnp.concatenate([first, second], axis=0)

    lanes = lax.broadcasted_iota(jnp.int32, (8, 128), 1)
    per_block = width // GROUP
    subs = CORES * local // 8

    def pack_scales(op):
        all_s = both_cores(own_s[op], peer_s[op])
        for b in range(OWNERS):
            tile = 2 * b * per_block // 128
            first = (2 * b * per_block) % 128
            packed = jnp.zeros((8, 128), F32)
            for sub in range(subs):
                part = all_s[sub * 8 : sub * 8 + 8, tile * 128 : tile * 128 + 128]
                shift = (sub * per_block + 256 - first - core * per_block) % 128
                part = pltpu.roll(part, shift, 1)
                mine = (lanes >= sub * per_block) & (lanes < (sub + 1) * per_block)
                packed = jnp.where(mine, part, packed)
            send_s[op, b] = packed

    def pack(op, i):
        @pl.loop(0, OWNERS)
        def _(b):
            parts = []
            for h in range(2):
                part = pl.ds(i * CHUNK + h * HALF, HALF)
                parts.append(both_cores(own_q[op, b, :, part], peer_q[op, b, :, part]))
            send_q[i, op, b] = jnp.concatenate(parts, axis=0).astype(BF16)

    def scatter(op, i):
        for slot in range(1, OWNERS):
            remote(
                leaving(op, i).at[owner(op, slot)], inbox(op, i).at[0, slot],
                s1_send.at[op, i], s1_recv.at[op, i], device(*group(op, slot), core),
            ).start()
        if i in DIRECT:
            for slot in range(OWNERS):
                remote(
                    leaving(op, i).at[owner(op, slot)], inbox(op, i).at[1, slot],
                    ex_send.at[op, i], ex_recv.at[op, i], device(*group(op, slot, 1), core),
                ).start()
        pltpu.make_async_copy(
            leaving(op, i).at[owner(op, 0)], inbox(op, i).at[0, 0], own_sem.at[op, i]
        ).start()

    def gathered(op, i):
        wait_for(inbox(op, i).at[0, pl.ds(1, OWNERS - 1)], s1_recv.at[op, i])
        wait_for(inbox(op, i).at[0, 0], own_sem.at[op, i])

    def exchange(op, i):
        if i not in DIRECT:
            gathered(op, i)
            remote(
                inbox(op, i).at[0], inbox(op, i).at[1],
                ex_send.at[op, i], ex_recv.at[op, i], partner[op],
            ).start()

    def spread(op, i):
        if i in DIRECT:
            gathered(op, i)
        wait_for(inbox(op, i).at[1], ex_recv.at[op, i])
        if i == chunks:
            for slot in range(OWNERS):
                raw_s[op, 0, slot] = first_s[op, 0, slot] + pltpu.roll(
                    first_s[op, 1, slot], terms, 1
                )
        for d, step in enumerate((1, -1)):
            remote(
                slab(op, i, 0), slab(op, i, step),
                s2_send.at[op, i, d], s2_recv.at[op, i, d], along(op, step),
            ).start()

    def forward(op, i):
        for d, step in enumerate((1, -1)):
            wait_for(slab(op, i, step), s2_recv.at[op, i, d])
            remote(
                half(op, i, step, d), half(op, i, 2, d),
                s3_send.at[op, i, d], s3_recv.at[op, i, d], along(op, step),
            ).start()

    def arrived(op, i):
        for d in range(2):
            wait_for(half(op, i, 2, d), s3_recv.at[op, i, d])

    terms = subs * per_block

    def make_pick():
        row = lax.broadcasted_iota(jnp.int32, (256, 128), 0)
        for i in range(chunks):
            for h in range(2):
                for sub in range(subs):
                    lane = sub * per_block + 2 * i + h
                    one = (row == lane) | (row == terms + lane) | (row == 128 + lane)
                    at = (h * subs + sub) * 128
                    pick[i, :, at : at + 128] = jnp.where(one, 1.0, 0.0).astype(BF16)

    def split_scales(op):
        n = OWNERS * 8
        lane = lax.broadcasted_iota(jnp.int32, (n, 128), 1)
        for step in range(RING):
            both_sides = raw_s[op, step].reshape(n, 128)
            for side in range(2):
                s = pltpu.roll(both_sides, 128 - terms, 1) if side else both_sides
                s = jnp.where(lane < terms, s, 0.0)
                high = s.astype(BF16).astype(F32)
                middle = (s - high).astype(BF16).astype(F32)
                low = (s - high) - middle
                at = pl.ds((step * 2 + side) * n, n)
                split_s[op, at, :128] = (high + pltpu.roll(middle, terms, 1)).astype(BF16)
                split_s[op, at, 128:] = low.astype(BF16)

    def expand(op, i):
        for n in range(0, wide_s.shape[2], 256):
            wide_s[wide(op, i), :, n : n + 256] = jnp.dot(
                split_s[op], pick[i, :, n : n + 256], preferred_element_type=F32
            )

    def wide(op, i):
        return 1 + op if i == chunks - 1 else 0

    def standardize(op, i):
        if i < chunks - 1:
            expand(op, i)

        def add(p, carry):
            sums, squares = list(carry[0]), list(carry[1])
            parts = [[], []]
            for q in range(OWNERS):
                block = raw[i, op, p // 2, p % 2, q].astype(F32)
                at = p * OWNERS + q
                if op == ADJ:
                    at = (q // 2) * 16 + (q % 2) * 8 + p
                part = pl.ds(pl.multiple_of(at * local_pair, 8), local_pair)
                s = pl.ds(pl.multiple_of((p * OWNERS + q) * 8, 8), 8)
                for h in range(2):
                    mine = [
                        block[n * 8 : n * 8 + 8] * wide_s[wide(op, i), s, n * 128 : n * 128 + 128]
                        for n in range(h * subs, (h + 1) * subs)
                    ]
                    work[part, h * HALF : (h + 1) * HALF] = jnp.concatenate(mine, axis=0)
                    parts[h] += mine
            for h in range(2):
                v = parts[h]
                w = [u * u for u in v]
                while len(v) > 1:
                    v = [sum(v[j : j + 2][1:], v[j]) for j in range(0, len(v), 2)]
                    w = [sum(w[j : j + 2][1:], w[j]) for j in range(0, len(w), 2)]
                sums[h] = sums[h] + v[0]
                squares[h] = squares[h] + w[0]
            return tuple(sums), tuple(squares)

        zero = jnp.zeros((8, HALF), F32)
        sums, squares = lax.fori_loop(
            0, CHIPS // OWNERS, add, ((zero, zero), (zero, zero)), unroll=2
        )
        average, factor = [], []
        for h in range(2):
            a = jnp.sum(sums[h], axis=0, keepdims=True) / tokens
            spread_ = jnp.sum(squares[h], axis=0, keepdims=True) / tokens - a * a
            average.append(a)
            factor.append(lax.rsqrt(spread_ + 1e-06) * (1.0 / math.sqrt(tokens)))

        rows = 128 if op == BASE else 96

        @pl.loop(0, tokens // rows, unroll=3 if op == BASE else 4)
        def _(t):
            part = pl.ds(pl.multiple_of(t * rows, rows), rows)
            for h in range(2):
                u = (work[part, h * HALF : (h + 1) * HALF] - average[h]) * factor[h]
                column = slice(i * CHUNK + h * HALF, i * CHUNK + (h + 1) * HALF)
                if op == BASE:
                    base_t[column, part] = u.astype(BF16).T
                else:
                    adj_u[core, part, column] = u.astype(BF16)

    swapped = set()

    traded = set()

    def depart(op, i):
        if op not in traded:
            traded.add(op)
            wait_for(peer_q.at[op], s0_recv.at[op])
            wait_for(peer_s.at[op], s0_recv.at[2 + op])
        if i < chunks:
            pack(op, i)
        else:
            pack_scales(op)
        scatter(op, i)

    def settle(op, i):
        arrived(op, i)
        if i == chunks:
            split_scales(op)
            return
        standardize(op, i)
        if op == ADJ:
            mine = adj_u.at[core, :, pl.ds(i * CHUNK, CHUNK)]
            remote(mine, mine, swap_send.at[i], swap_recv.at[i], peer).start()
        if i == 0:
            expand(op, chunks - 1)

    def multiply(part, i):
        if i not in swapped:
            swapped.add(i)
            wait_for(adj_u.at[other, :, pl.ds(i * CHUNK, CHUNK)], swap_recv.at[i])

        @pl.loop(0, CORES)
        def _(half):
            (columns, rows)[part](base_t, adj_u, early, i, i * CHUNK, half)

    stage = {
        "d": depart, "e": exchange, "s": spread, "f": forward, "t": settle, "m": multiply,
    }
    for word in " ".join(ORDER).split():
        if word == "pick":
            make_pick()
        elif word != "m0b":
            stage[word[0]]("BA".index(word[2]) if word[0] != "m" else "ab".index(word[2]), int(word[1]))
    i = chunks - 1
    wait_for(adj_u.at[other, :, pl.ds(i * CHUNK, CHUNK)], swap_recv.at[i])

    for op in (BASE, ADJ):
        wait_for(peer_q.at[op], s0_send.at[op])
        wait_for(peer_s.at[op], s0_send.at[2 + op])
        for i in range(chunks + 1):
            wait_for(inbox(op, i).at[0, pl.ds(1, OWNERS - 1)], s1_send.at[op, i])
            wait_for(inbox(op, i).at[0], ex_send.at[op, i])
            for d in range(2):
                wait_for(slab(op, i, 0), s2_send.at[op, i, d])
                wait_for(half(op, i, 0, 0), s3_send.at[op, i, d])
    for i in range(chunks):
        wait_for(adj_u.at[core, :, pl.ds(i * CHUNK, CHUNK)], swap_send.at[i])


def gather(base_q, base_s, adj_q, adj_s):
    local, latents = base_q.shape
    width = latents // (OWNERS * CORES)
    chunks = width // CHUNK
    early = width - CHUNK
    tokens = local * CORES * RING**3
    rows = 2 * CORES * local
    subs = CORES * local // 8
    dma = pltpu.SemaphoreType.DMA
    whole = pl.BlockSpec(memory_space=VMEM)
    return pl.pallas_call(
        functools.partial(gather_kernel, local, width),
        out_shape=(
            VMEM((width, tokens), BF16),
            VMEM((CORES, tokens, width), BF16),
            VMEM((CORES, early, early), BF16),
        ),
        in_specs=[pl.BlockSpec(memory_space=pltpu.HBM)] * 4,
        out_specs=(whole,) * 3,
        scratch_shapes=[
            VMEM((2, OWNERS, local, width), BF16),
            VMEM((2,) + base_s.shape, F32),
            VMEM((2, OWNERS, local, width), BF16),
            VMEM((2,) + base_s.shape, F32),
            VMEM((chunks, 2, OWNERS, rows, HALF), BF16),
            VMEM((2, OWNERS, 8, 128), F32),
            VMEM((chunks, 2, RING, 2, OWNERS, rows, HALF), BF16),
            VMEM((2, 2, OWNERS, 8, 128), F32),
            VMEM((2, RING, OWNERS, 8, 128), F32),
            VMEM((2, CHIPS * 8, 256), BF16),
            VMEM((chunks, 256, 2 * subs * 128), BF16),
            VMEM((3, CHIPS * 8, 2 * subs * 128), F32),
            VMEM((tokens, CHUNK), F32),
            dma((2, OWNERS + 1)),
            dma((4,)), dma((4,)),
            dma((2, chunks + 1)), dma((2, chunks + 1)),
            dma((2, chunks + 1)), dma((2, chunks + 1)),
            dma((2, chunks + 1, 2)), dma((2, chunks + 1, 2)),
            dma((2, chunks + 1, 2)), dma((2, chunks + 1, 2)),
            dma((2, chunks + 1)),
            dma((chunks,)), dma((chunks,)),
        ],
        compiler_params=pltpu.CompilerParams(
            collective_id=0, has_side_effects=True, vmem_limit_bytes=30 << 20
        ),
        name="gather_units",
    )(base_q, base_s, adj_q, adj_s)


def product_kernel(base_t, adj_u, early, out, below, beside, early_sem, late_sem):
    width = base_t.shape[0]
    done_to = early.shape[1]
    moves = [
        pltpu.make_async_copy(
            early.at[half, a : a + CHUNK],
            out.at[a : a + CHUNK, half * width : half * width + done_to],
            early_sem.at[half, a // CHUNK],
        )
        for half in range(CORES)
        for a in range(0, done_to, CHUNK)
    ]
    for move in moves:
        move.start()

    def late(half, which):
        start = pl.multiple_of(half * width, width)
        if which == 0:
            at = out.at[:, pl.ds(start + done_to, CHUNK)]
            return pltpu.make_async_copy(below.at[half], at, late_sem.at[half, 0])
        at = out.at[pl.ds(done_to, CHUNK), pl.ds(start, done_to)]
        return pltpu.make_async_copy(beside.at[half], at, late_sem.at[half, 1])

    @pl.loop(0, CORES)
    def _(half):
        columns(base_t, adj_u, below, done_to // CHUNK, 0, half)
        late(half, 0).start()
        rows(base_t, adj_u, beside, done_to // CHUNK, 0, half)
        late(half, 1).start()

    for half in range(CORES):
        for which in range(2):
            late(half, which).wait()
    for move in moves:
        move.wait()


def product(base_t, adj_u, early):
    width = base_t.shape[0]
    whole = pl.BlockSpec(memory_space=VMEM)
    return pl.pallas_call(
        product_kernel,
        out_shape=jax.ShapeDtypeStruct((width, CORES * width), BF16),
        in_specs=[whole] * 3,
        out_specs=pl.BlockSpec(memory_space=pl.ANY),
        scratch_shapes=[
            VMEM((CORES, width, CHUNK), BF16),
            VMEM((CORES, CHUNK, width - CHUNK), BF16),
            pltpu.SemaphoreType.DMA((CORES, width // CHUNK - 1)),
            pltpu.SemaphoreType.DMA((CORES, 2)),
        ],
        compiler_params=pltpu.CompilerParams(vmem_limit_bytes=8 << 20),
        name="correlate",
    )(base_t, adj_u, early)


def on_device(*args):
    units = gather(*args)
    return product(*(pltpu.with_memory_space_constraint(u, VMEM) for u in units))


def solution(mesh):
    spec = P(("row", "col"), None)
    return jax.shard_map(
        on_device, mesh=mesh, in_specs=(spec,) * 4, out_specs=P("row", "col"), check_vma=False
    )
```

```python
import functools
import math

import jax
import jax.numpy as jnp
from jax import lax
from jax.experimental import pallas as pl
from jax.experimental.pallas import tpu as pltpu
from jax.sharding import PartitionSpec as P

MESH = pl.DeviceIdType.MESH
VMEM = pltpu.VMEM
BF16 = jnp.bfloat16
F32 = jnp.float32

CORES = 2
RING = 4
GROUP = 128
OWNERS = 8
CHIPS = RING * 2 * OWNERS
BASE, ADJ = 0, 1
CHUNK = 256
HALF = CHUNK // 2
DIRECT = (0, 8)


ORDER = (
    "d1B d1A d0A d2B",
    "d8A d8B d0B e1A",
    "pick e1B d4B d4A",
    "s0A s8A d2A d3A",
    "d3B s0B s8B s1A",
    "s1B e2B f0A f8A",
    "e2A d5B f0B f8B",
    "d6B f1A e3A e3B",
    "d5A e4A d7B s2B",
    "s2A t8A t0A e4B",
    "d6A f1B d7A t1A",
    "s3A f2B s3B t8B",
    "t0B m0a e5A f2A",
    "s4A t1B f3A e5B",
    "s4B t2B t2A e6A",
    "m1a s5A e7A f3B",
    "e6B e7B m2a s5B",
    "f4A m1b t3A s6A",
    "m2b f4B t3B m3a",
    "f5A s6B s7A t4A",
    "m3b f5B t4B m4a",
    "f6A t5A s7B f6B",
    "m4b t5B f7A m5b",
    "t6A m0b m5a f7B",
    "t6B m6a t7A m6b",
    "t7B",
)

EARLY = 2


def place():
    row, col = lax.axis_index("row"), lax.axis_index("col")
    x, z_hi = col // 2, col % 2
    y, z_lo, core = row // 4, (row // 2) % 2, row % 2
    return x, y, z_hi * 2 + z_lo, core


def device(x, y, z, core):
    x, y, z = x % RING, y % RING, z % RING
    return (y * 2 + z % 2) * CORES + core, x * 2 + z // 2


def pieces(n, most):
    count = max(1, -(-n // most))
    edges = [n // CHUNK * j // count * CHUNK for j in range(count + 1)]
    return [(a, b - a) for a, b in zip(edges, edges[1:]) if b > a]


def columns(base_t, adj_u, out, i, at, half):
    new = slice(i * CHUNK, (i + 1) * CHUNK)
    for a, n in pieces((i + 1) * CHUNK, 1024):
        out[half, a : a + n, at : at + CHUNK] = jnp.dot(
            base_t[a : a + n, :], adj_u[half, :, new], preferred_element_type=F32
        ).astype(BF16)


def rows(base_t, adj_u, out, i, at, half):
    new = slice(i * CHUNK, (i + 1) * CHUNK)
    for a, n in pieces(i * CHUNK, 1024):
        out[half, at : at + CHUNK, a : a + n] = jnp.dot(
            base_t[new, :], adj_u[half, :, a : a + n], preferred_element_type=F32
        ).astype(BF16)


def gather_kernel(
    local, width,
    base_q, base_s, adj_q, adj_s,
    base_t, adj_u, early,
    own_q, own_s, peer_q, peer_s, send_q, send_s, raw, first_s, raw_s,
    split_s, pick, wide_s, work,
    load_sem, s0_send, s0_recv, s1_send, s1_recv, ex_send, ex_recv, s2_send, s2_recv, s3_send, s3_recv,
    own_sem, swap_send, swap_recv,
):
    x, y, z, core = place()
    other = 1 - core
    chunks = width // CHUNK
    tokens = adj_u.shape[1]
    local_pair = CORES * local
    queue = (base_q, adj_q)
    scale = (base_s, adj_s)
    peer = device(x, y, z, other)

    near, far = z + 1 - 2 * (z % 2), z + 2

    def group(op, slot, side=0):
        step, across = slot // 2, slot % 2
        if op == BASE:
            return x, y + step, (near if across else z) + 2 * side
        return x + step, y, (far if across else z) + (near - z) * side

    def owner(op, slot):
        px, py, pz = group(op, slot)
        if op == BASE:
            return (py % RING) * 2 + pz % 2
        return (px % RING) * 2 + (pz % RING) // 2

    partner = (device(x, y, far, core), device(x, y, near, core))

    def along(op, step):
        return device(x + step, y, z, core) if op == BASE else device(x, y + step, z, core)

    def inbox(op, i):
        return first_s.at[op] if i == chunks else raw.at[i, op, 0]

    def slab(op, i, step):
        return raw_s.at[op, step % RING] if i == chunks else raw.at[i, op, step % RING]

    def half(op, i, step, d):
        if i == chunks:
            return raw_s.at[op, step % RING, pl.ds(d * (OWNERS // 2), OWNERS // 2)]
        return raw.at[i, op, step % RING, d]

    def leaving(op, i):
        return send_s.at[op] if i == chunks else send_q.at[i, op]

    def remote(src, dst, send_sem, recv_sem, where):
        return pltpu.make_async_remote_copy(
            src_ref=src, dst_ref=dst, send_sem=send_sem, recv_sem=recv_sem,
            device_id=where, device_id_type=MESH,
        )

    def wait_for(ref, sem):
        pltpu.make_async_copy(ref, ref, sem).wait()

    loads = []
    for op in (BASE, ADJ):
        for b in range(OWNERS):
            start = pl.multiple_of((2 * b + core) * width, width)
            loads.append(
                pltpu.make_async_copy(
                    queue[op].at[:, pl.ds(start, width)], own_q.at[op, b], load_sem.at[op, b]
                )
            )
        loads.append(pltpu.make_async_copy(scale[op], own_s.at[op], load_sem.at[op, OWNERS]))
    for load in loads:
        load.start()

    barrier = pltpu.get_barrier_semaphore()
    greeted = [peer]
    for slot in range(1, OWNERS):
        greeted += [device(*group(op, slot), core) for op in (BASE, ADJ)]
        greeted += [device(*group(op, slot, 1), core) for op in (BASE, ADJ)[: slot]]
    for where in greeted:
        pl.semaphore_signal(barrier, inc=1, device_id=where, device_id_type=MESH)
    pl.semaphore_wait(barrier, len(greeted))

    for op in (BASE, ADJ):
        for b in range(OWNERS):
            start = pl.multiple_of((2 * b + other) * width, width)
            remote(
                queue[op].at[:, pl.ds(start, width)], peer_q.at[op, b],
                s0_send.at[op], s0_recv.at[op], peer,
            ).start()
        remote(scale[op], peer_s.at[op], s0_send.at[2 + op], s0_recv.at[2 + op], peer).start()
    for load in loads:
        load.wait()

    def both_cores(own, theirs):
        own, theirs = own.astype(F32), theirs.astype(F32)
        first = jnp.where(core == 0, own, theirs)
        second = jnp.where(core == 0, theirs, own)
        return jnp.concatenate([first, second], axis=0)

    lanes = lax.broadcasted_iota(jnp.int32, (8, 128), 1)
    per_block = width // GROUP
    subs = CORES * local // 8

    def pack_scales(op):
        all_s = both_cores(own_s[op], peer_s[op])
        for b in range(OWNERS):
            tile = 2 * b * per_block // 128
            first = (2 * b * per_block) % 128
            packed = jnp.zeros((8, 128), F32)
            for sub in range(subs):
                part = all_s[sub * 8 : sub * 8 + 8, tile * 128 : tile * 128 + 128]
                shift = (sub * per_block + 256 - first - core * per_block) % 128
                part = pltpu.roll(part, shift, 1)
                mine = (lanes >= sub * per_block) & (lanes < (sub + 1) * per_block)
                packed = jnp.where(mine, part, packed)
            send_s[op, b] = packed

    def pack(op, i):
        @pl.loop(0, OWNERS)
        def _(b):
            parts = []
            for h in range(2):
                part = pl.ds(i * CHUNK + h * HALF, HALF)
                parts.append(both_cores(own_q[op, b, :, part], peer_q[op, b, :, part]))
            send_q[i, op, b] = jnp.concatenate(parts, axis=0).astype(BF16)

    def scatter(op, i):
        for slot in range(1, OWNERS):
            remote(
                leaving(op, i).at[owner(op, slot)], inbox(op, i).at[0, slot],
                s1_send.at[op, i], s1_recv.at[op, i], device(*group(op, slot), core),
            ).start()
        if i in DIRECT:
            for slot in range(OWNERS):
                remote(
                    leaving(op, i).at[owner(op, slot)], inbox(op, i).at[1, slot],
                    ex_send.at[op, i], ex_recv.at[op, i], device(*group(op, slot, 1), core),
                ).start()
        pltpu.make_async_copy(
            leaving(op, i).at[owner(op, 0)], inbox(op, i).at[0, 0], own_sem.at[op, i]
        ).start()

    def gathered(op, i):
        wait_for(inbox(op, i).at[0, pl.ds(1, OWNERS - 1)], s1_recv.at[op, i])
        wait_for(inbox(op, i).at[0, 0], own_sem.at[op, i])

    def exchange(op, i):
        if i not in DIRECT:
            gathered(op, i)
            remote(
                inbox(op, i).at[0], inbox(op, i).at[1],
                ex_send.at[op, i], ex_recv.at[op, i], partner[op],
            ).start()

    def spread(op, i):
        if i in DIRECT:
            gathered(op, i)
        wait_for(inbox(op, i).at[1], ex_recv.at[op, i])
        if i == chunks:
            for slot in range(OWNERS):
                raw_s[op, 0, slot] = first_s[op, 0, slot] + pltpu.roll(
                    first_s[op, 1, slot], terms, 1
                )
        for d, step in enumerate((1, -1)):
            remote(
                slab(op, i, 0), slab(op, i, step),
                s2_send.at[op, i, d], s2_recv.at[op, i, d], along(op, step),
            ).start()

    def forward(op, i):
        for d, step in enumerate((1, -1)):
            wait_for(slab(op, i, step), s2_recv.at[op, i, d])
            remote(
                half(op, i, step, d), half(op, i, 2, d),
                s3_send.at[op, i, d], s3_recv.at[op, i, d], along(op, step),
            ).start()

    def arrived(op, i):
        for d in range(2):
            wait_for(half(op, i, 2, d), s3_recv.at[op, i, d])

    terms = subs * per_block

    def make_pick():
        row = lax.broadcasted_iota(jnp.int32, (256, 128), 0)
        for i in range(chunks):
            for h in range(2):
                for sub in range(subs):
                    lane = sub * per_block + 2 * i + h
                    one = (row == lane) | (row == terms + lane) | (row == 128 + lane)
                    at = (h * subs + sub) * 128
                    pick[i, :, at : at + 128] = jnp.where(one, 1.0, 0.0).astype(BF16)

    def split_scales(op):
        n = OWNERS * 8
        lane = lax.broadcasted_iota(jnp.int32, (n, 128), 1)
        for step in range(RING):
            both_sides = raw_s[op, step].reshape(n, 128)
            for side in range(2):
                s = pltpu.roll(both_sides, 128 - terms, 1) if side else both_sides
                s = jnp.where(lane < terms, s, 0.0)
                high = s.astype(BF16).astype(F32)
                middle = (s - high).astype(BF16).astype(F32)
                low = (s - high) - middle
                at = pl.ds((step * 2 + side) * n, n)
                split_s[op, at, :128] = (high + pltpu.roll(middle, terms, 1)).astype(BF16)
                split_s[op, at, 128:] = low.astype(BF16)

    def expand(op, i):
        for n in range(0, wide_s.shape[2], 256):
            wide_s[wide(op, i), :, n : n + 256] = jnp.dot(
                split_s[op], pick[i, :, n : n + 256], preferred_element_type=F32
            )

    def wide(op, i):
        ahead = i - (chunks - EARLY)
        return 1 + 2 * ahead + op if ahead >= 0 else 0

    def standardize(op, i):
        if i < chunks - EARLY:
            expand(op, i)

        def add(p, carry):
            sums, squares = list(carry[0]), list(carry[1])
            parts = [[], []]
            for q in range(OWNERS):
                block = raw[i, op, p // 2, p % 2, q].astype(F32)
                at = p * OWNERS + q
                if op == ADJ:
                    at = (q // 2) * 16 + (q % 2) * 8 + p
                part = pl.ds(pl.multiple_of(at * local_pair, 8), local_pair)
                s = pl.ds(pl.multiple_of((p * OWNERS + q) * 8, 8), 8)
                for h in range(2):
                    mine = [
                        block[n * 8 : n * 8 + 8] * wide_s[wide(op, i), s, n * 128 : n * 128 + 128]
                        for n in range(h * subs, (h + 1) * subs)
                    ]
                    work[part, h * HALF : (h + 1) * HALF] = jnp.concatenate(mine, axis=0)
                    parts[h] += mine
            for h in range(2):
                v = parts[h]
                w = [u * u for u in v]
                while len(v) > 1:
                    v = [sum(v[j : j + 2][1:], v[j]) for j in range(0, len(v), 2)]
                    w = [sum(w[j : j + 2][1:], w[j]) for j in range(0, len(w), 2)]
                sums[h] = sums[h] + v[0]
                squares[h] = squares[h] + w[0]
            return tuple(sums), tuple(squares)

        zero = jnp.zeros((8, HALF), F32)
        sums, squares = lax.fori_loop(
            0, CHIPS // OWNERS, add, ((zero, zero), (zero, zero)), unroll=2
        )
        average, factor = [], []
        for h in range(2):
            a = jnp.sum(sums[h], axis=0, keepdims=True) / tokens
            spread_ = jnp.sum(squares[h], axis=0, keepdims=True) / tokens - a * a
            average.append(a)
            factor.append(lax.rsqrt(spread_ + 1e-06) * (1.0 / math.sqrt(tokens)))

        rows = 128 if op == BASE else 96

        @pl.loop(0, tokens // rows, unroll=3 if op == BASE else 4)
        def _(t):
            part = pl.ds(pl.multiple_of(t * rows, rows), rows)
            for h in range(2):
                u = (work[part, h * HALF : (h + 1) * HALF] - average[h]) * factor[h]
                column = slice(i * CHUNK + h * HALF, i * CHUNK + (h + 1) * HALF)
                if op == BASE:
                    base_t[column, part] = u.astype(BF16).T
                else:
                    adj_u[core, part, column] = u.astype(BF16)

    swapped = set()

    traded = set()

    def depart(op, i):
        if op not in traded:
            traded.add(op)
            wait_for(peer_q.at[op], s0_recv.at[op])
            wait_for(peer_s.at[op], s0_recv.at[2 + op])
        if i < chunks:
            pack(op, i)
        else:
            pack_scales(op)
        scatter(op, i)

    def settle(op, i):
        arrived(op, i)
        if i == chunks:
            split_scales(op)
            return
        standardize(op, i)
        if op == ADJ:
            mine = adj_u.at[core, :, pl.ds(i * CHUNK, CHUNK)]
            remote(mine, mine, swap_send.at[i], swap_recv.at[i], peer).start()
        if i < EARLY:
            expand(op, chunks - 1 - i)

    def multiply(part, i):
        if i not in swapped:
            swapped.add(i)
            wait_for(adj_u.at[other, :, pl.ds(i * CHUNK, CHUNK)], swap_recv.at[i])

        @pl.loop(0, CORES)
        def _(half):
            (columns, rows)[part](base_t, adj_u, early, i, i * CHUNK, half)

    stage = {
        "d": depart, "e": exchange, "s": spread, "f": forward, "t": settle, "m": multiply,
    }
    for word in " ".join(ORDER).split():
        if word == "pick":
            make_pick()
        elif word != "m0b":
            stage[word[0]]("BA".index(word[2]) if word[0] != "m" else "ab".index(word[2]), int(word[1]))
    i = chunks - 1
    wait_for(adj_u.at[other, :, pl.ds(i * CHUNK, CHUNK)], swap_recv.at[i])

    for op in (BASE, ADJ):
        wait_for(peer_q.at[op], s0_send.at[op])
        wait_for(peer_s.at[op], s0_send.at[2 + op])
        for i in range(chunks + 1):
            wait_for(inbox(op, i).at[0, pl.ds(1, OWNERS - 1)], s1_send.at[op, i])
            wait_for(inbox(op, i).at[0], ex_send.at[op, i])
            for d in range(2):
                wait_for(slab(op, i, 0), s2_send.at[op, i, d])
                wait_for(half(op, i, 0, 0), s3_send.at[op, i, d])
    for i in range(chunks):
        wait_for(adj_u.at[core, :, pl.ds(i * CHUNK, CHUNK)], swap_send.at[i])


def gather(base_q, base_s, adj_q, adj_s):
    local, latents = base_q.shape
    width = latents // (OWNERS * CORES)
    chunks = width // CHUNK
    early = width - CHUNK
    tokens = local * CORES * RING**3
    rows = 2 * CORES * local
    subs = CORES * local // 8
    dma = pltpu.SemaphoreType.DMA
    whole = pl.BlockSpec(memory_space=VMEM)
    return pl.pallas_call(
        functools.partial(gather_kernel, local, width),
        out_shape=(
            VMEM((width, tokens), BF16),
            VMEM((CORES, tokens, width), BF16),
            VMEM((CORES, early, early), BF16),
        ),
        in_specs=[pl.BlockSpec(memory_space=pltpu.HBM)] * 4,
        out_specs=(whole,) * 3,
        scratch_shapes=[
            VMEM((2, OWNERS, local, width), BF16),
            VMEM((2,) + base_s.shape, F32),
            VMEM((2, OWNERS, local, width), BF16),
            VMEM((2,) + base_s.shape, F32),
            VMEM((chunks, 2, OWNERS, rows, HALF), BF16),
            VMEM((2, OWNERS, 8, 128), F32),
            VMEM((chunks, 2, RING, 2, OWNERS, rows, HALF), BF16),
            VMEM((2, 2, OWNERS, 8, 128), F32),
            VMEM((2, RING, OWNERS, 8, 128), F32),
            VMEM((2, CHIPS * 8, 256), BF16),
            VMEM((chunks, 256, 2 * subs * 128), BF16),
            VMEM((1 + 2 * EARLY, CHIPS * 8, 2 * subs * 128), F32),
            VMEM((tokens, CHUNK), F32),
            dma((2, OWNERS + 1)),
            dma((4,)), dma((4,)),
            dma((2, chunks + 1)), dma((2, chunks + 1)),
            dma((2, chunks + 1)), dma((2, chunks + 1)),
            dma((2, chunks + 1, 2)), dma((2, chunks + 1, 2)),
            dma((2, chunks + 1, 2)), dma((2, chunks + 1, 2)),
            dma((2, chunks + 1)),
            dma((chunks,)), dma((chunks,)),
        ],
        compiler_params=pltpu.CompilerParams(
            collective_id=0, has_side_effects=True, vmem_limit_bytes=30 << 20
        ),
        name="gather_units",
    )(base_q, base_s, adj_q, adj_s)


def product_kernel(base_t, adj_u, early, out, below, beside, early_sem, late_sem):
    width = base_t.shape[0]
    done_to = early.shape[1]
    moves = [
        pltpu.make_async_copy(
            early.at[half, a : a + CHUNK],
            out.at[a : a + CHUNK, half * width : half * width + done_to],
            early_sem.at[half, a // CHUNK],
        )
        for half in range(CORES)
        for a in range(0, done_to, CHUNK)
    ]
    for move in moves:
        move.start()

    def late(half, which):
        start = pl.multiple_of(half * width, width)
        if which == 0:
            at = out.at[:, pl.ds(start + done_to, CHUNK)]
            return pltpu.make_async_copy(below.at[half], at, late_sem.at[half, 0])
        at = out.at[pl.ds(done_to, CHUNK), pl.ds(start, done_to)]
        return pltpu.make_async_copy(beside.at[half], at, late_sem.at[half, 1])

    @pl.loop(0, CORES)
    def _(half):
        columns(base_t, adj_u, below, done_to // CHUNK, 0, half)
        late(half, 0).start()
        rows(base_t, adj_u, beside, done_to // CHUNK, 0, half)
        late(half, 1).start()

    for half in range(CORES):
        for which in range(2):
            late(half, which).wait()
    for move in moves:
        move.wait()


def product(base_t, adj_u, early):
    width = base_t.shape[0]
    whole = pl.BlockSpec(memory_space=VMEM)
    return pl.pallas_call(
        product_kernel,
        out_shape=jax.ShapeDtypeStruct((width, CORES * width), BF16),
        in_specs=[whole] * 3,
        out_specs=pl.BlockSpec(memory_space=pl.ANY),
        scratch_shapes=[
            VMEM((CORES, width, CHUNK), BF16),
            VMEM((CORES, CHUNK, width - CHUNK), BF16),
            pltpu.SemaphoreType.DMA((CORES, width // CHUNK - 1)),
            pltpu.SemaphoreType.DMA((CORES, 2)),
        ],
        compiler_params=pltpu.CompilerParams(vmem_limit_bytes=8 << 20),
        name="correlate",
    )(base_t, adj_u, early)


def on_device(*args):
    units = gather(*args)
    return product(*(pltpu.with_memory_space_constraint(u, VMEM) for u in units))


def solution(mesh):
    spec = P(("row", "col"), None)
    return jax.shard_map(
        on_device, mesh=mesh, in_specs=(spec,) * 4, out_specs=P("row", "col"), check_vma=False
    )
```

```python
import functools
import math

import jax
import jax.numpy as jnp
from jax import lax
from jax.experimental import pallas as pl
from jax.experimental.pallas import tpu as pltpu
from jax.sharding import PartitionSpec as P

MESH = pl.DeviceIdType.MESH
VMEM = pltpu.VMEM
BF16 = jnp.bfloat16
F32 = jnp.float32

CORES = 2
RING = 4
GROUP = 128
OWNERS = 8
CHIPS = RING * 2 * OWNERS
BASE, ADJ = 0, 1
CHUNK = 256
HALF = CHUNK // 2
DIRECT = (0, 8)


ORDER = (
    "d1B d1A d0A d2B",
    "d8A d8B d0B e1A",
    "pick e1B d4B d4A",
    "s0A s8A d2A d3A",
    "s0B s8B e2B d3B",
    "s1A s1B f0A f8A",
    "e2A d6B e3A f0B",
    "f8B d7B f1A d5B",
    "s2B d5A e3B s2A",
    "f1B e4A t8B t0B",
    "e4B t8A t0A s3A",
    "d6A f2B t1A d7A",
    "f2A m0a e5A s3B",
    "e5B t1B s4A m1a",
    "t2B s4B f3A m1b",
    "t2A e6A e6B e7A",
    "e7B s5A f3B m2a",
    "f4A s5B t3A m2b",
    "s6A f4B t3B s6B",
    "m3a f5A s7A m0b",
    "t4A m3b f5B t4B",
    "s7B m4a t5A f6A",
    "m4b f6B f7A t5B",
    "m5b t6A m5a t6B",
    "f7B m6a t7A m6b",
    "t7B",
)

EARLY = 3


def place():
    row, col = lax.axis_index("row"), lax.axis_index("col")
    x, z_hi = col // 2, col % 2
    y, z_lo, core = row // 4, (row // 2) % 2, row % 2
    return x, y, z_hi * 2 + z_lo, core


def device(x, y, z, core):
    x, y, z = x % RING, y % RING, z % RING
    return (y * 2 + z % 2) * CORES + core, x * 2 + z // 2


def pieces(n, most):
    count = max(1, -(-n // most))
    edges = [n // CHUNK * j // count * CHUNK for j in range(count + 1)]
    return [(a, b - a) for a, b in zip(edges, edges[1:]) if b > a]


def columns(base_t, adj_u, out, i, at, half):
    new = slice(i * CHUNK, (i + 1) * CHUNK)
    for a, n in pieces((i + 1) * CHUNK, 1024):
        out[half, a : a + n, at : at + CHUNK] = jnp.dot(
            base_t[a : a + n, :], adj_u[half, :, new], preferred_element_type=F32
        ).astype(BF16)


def rows(base_t, adj_u, out, i, at, half):
    new = slice(i * CHUNK, (i + 1) * CHUNK)
    for a, n in pieces(i * CHUNK, 1024):
        out[half, at : at + CHUNK, a : a + n] = jnp.dot(
            base_t[new, :], adj_u[half, :, a : a + n], preferred_element_type=F32
        ).astype(BF16)


def gather_kernel(
    local, width,
    base_q, base_s, adj_q, adj_s,
    base_t, adj_u, early,
    own_q, own_s, peer_q, peer_s, send_q, send_s, raw, first_s, raw_s,
    split_s, pick, wide_s, work,
    load_sem, s0_send, s0_recv, s1_send, s1_recv, ex_send, ex_recv, s2_send, s2_recv, s3_send, s3_recv,
    own_sem, swap_send, swap_recv,
):
    x, y, z, core = place()
    other = 1 - core
    chunks = width // CHUNK
    tokens = adj_u.shape[1]
    local_pair = CORES * local
    queue = (base_q, adj_q)
    scale = (base_s, adj_s)
    peer = device(x, y, z, other)

    near, far = z + 1 - 2 * (z % 2), z + 2

    def group(op, slot, side=0):
        step, across = slot // 2, slot % 2
        if op == BASE:
            return x, y + step, (near if across else z) + 2 * side
        return x + step, y, (far if across else z) + (near - z) * side

    def owner(op, slot):
        px, py, pz = group(op, slot)
        if op == BASE:
            return (py % RING) * 2 + pz % 2
        return (px % RING) * 2 + (pz % RING) // 2

    partner = (device(x, y, far, core), device(x, y, near, core))

    def along(op, step):
        return device(x + step, y, z, core) if op == BASE else device(x, y + step, z, core)

    def inbox(op, i):
        return first_s.at[op] if i == chunks else raw.at[i, op, 0]

    def slab(op, i, step):
        return raw_s.at[op, step % RING] if i == chunks else raw.at[i, op, step % RING]

    def half(op, i, step, d):
        if i == chunks:
            return raw_s.at[op, step % RING, pl.ds(d * (OWNERS // 2), OWNERS // 2)]
        return raw.at[i, op, step % RING, d]

    def leaving(op, i):
        return send_s.at[op] if i == chunks else send_q.at[i, op]

    def remote(src, dst, send_sem, recv_sem, where):
        return pltpu.make_async_remote_copy(
            src_ref=src, dst_ref=dst, send_sem=send_sem, recv_sem=recv_sem,
            device_id=where, device_id_type=MESH,
        )

    def wait_for(ref, sem):
        pltpu.make_async_copy(ref, ref, sem).wait()

    loads = []
    for op in (BASE, ADJ):
        for b in range(OWNERS):
            start = pl.multiple_of((2 * b + core) * width, width)
            loads.append(
                pltpu.make_async_copy(
                    queue[op].at[:, pl.ds(start, width)], own_q.at[op, b], load_sem.at[op, b]
                )
            )
        loads.append(pltpu.make_async_copy(scale[op], own_s.at[op], load_sem.at[op, OWNERS]))
    for load in loads:
        load.start()

    barrier = pltpu.get_barrier_semaphore()
    greeted = [peer]
    for slot in range(1, OWNERS):
        greeted += [device(*group(op, slot), core) for op in (BASE, ADJ)]
        greeted += [device(*group(op, slot, 1), core) for op in (BASE, ADJ)[: slot]]
    for where in greeted:
        pl.semaphore_signal(barrier, inc=1, device_id=where, device_id_type=MESH)
    pl.semaphore_wait(barrier, len(greeted))

    for op in (BASE, ADJ):
        for b in range(OWNERS):
            start = pl.multiple_of((2 * b + other) * width, width)
            remote(
                queue[op].at[:, pl.ds(start, width)], peer_q.at[op, b],
                s0_send.at[op], s0_recv.at[op], peer,
            ).start()
        remote(scale[op], peer_s.at[op], s0_send.at[2 + op], s0_recv.at[2 + op], peer).start()
    for load in loads:
        load.wait()

    def both_cores(own, theirs):
        own, theirs = own.astype(F32), theirs.astype(F32)
        first = jnp.where(core == 0, own, theirs)
        second = jnp.where(core == 0, theirs, own)
        return jnp.concatenate([first, second], axis=0)

    lanes = lax.broadcasted_iota(jnp.int32, (8, 128), 1)
    per_block = width // GROUP
    subs = CORES * local // 8

    def pack_scales(op):
        all_s = both_cores(own_s[op], peer_s[op])
        for b in range(OWNERS):
            tile = 2 * b * per_block // 128
            first = (2 * b * per_block) % 128
            packed = jnp.zeros((8, 128), F32)
            for sub in range(subs):
                part = all_s[sub * 8 : sub * 8 + 8, tile * 128 : tile * 128 + 128]
                shift = (sub * per_block + 256 - first - core * per_block) % 128
                part = pltpu.roll(part, shift, 1)
                mine = (lanes >= sub * per_block) & (lanes < (sub + 1) * per_block)
                packed = jnp.where(mine, part, packed)
            send_s[op, b] = packed

    def pack(op, i):
        @pl.loop(0, OWNERS)
        def _(b):
            parts = []
            for h in range(2):
                part = pl.ds(i * CHUNK + h * HALF, HALF)
                parts.append(both_cores(own_q[op, b, :, part], peer_q[op, b, :, part]))
            send_q[i, op, b] = jnp.concatenate(parts, axis=0).astype(BF16)

    def scatter(op, i):
        for slot in range(1, OWNERS):
            remote(
                leaving(op, i).at[owner(op, slot)], inbox(op, i).at[0, slot],
                s1_send.at[op, i], s1_recv.at[op, i], device(*group(op, slot), core),
            ).start()
        if i in DIRECT:
            for slot in range(OWNERS):
                remote(
                    leaving(op, i).at[owner(op, slot)], inbox(op, i).at[1, slot],
                    ex_send.at[op, i], ex_recv.at[op, i], device(*group(op, slot, 1), core),
                ).start()
        pltpu.make_async_copy(
            leaving(op, i).at[owner(op, 0)], inbox(op, i).at[0, 0], own_sem.at[op, i]
        ).start()

    def gathered(op, i):
        wait_for(inbox(op, i).at[0, pl.ds(1, OWNERS - 1)], s1_recv.at[op, i])
        wait_for(inbox(op, i).at[0, 0], own_sem.at[op, i])

    def exchange(op, i):
        if i not in DIRECT:
            gathered(op, i)
            remote(
                inbox(op, i).at[0], inbox(op, i).at[1],
                ex_send.at[op, i], ex_recv.at[op, i], partner[op],
            ).start()

    def spread(op, i):
        if i in DIRECT:
            gathered(op, i)
        wait_for(inbox(op, i).at[1], ex_recv.at[op, i])
        if i == chunks:
            for slot in range(OWNERS):
                raw_s[op, 0, slot] = first_s[op, 0, slot] + pltpu.roll(
                    first_s[op, 1, slot], terms, 1
                )
        for d, step in enumerate((1, -1)):
            remote(
                slab(op, i, 0), slab(op, i, step),
                s2_send.at[op, i, d], s2_recv.at[op, i, d], along(op, step),
            ).start()

    def forward(op, i):
        for d, step in enumerate((1, -1)):
            wait_for(slab(op, i, step), s2_recv.at[op, i, d])
            remote(
                half(op, i, step, d), half(op, i, 2, d),
                s3_send.at[op, i, d], s3_recv.at[op, i, d], along(op, step),
            ).start()

    def arrived(op, i):
        for d in range(2):
            wait_for(half(op, i, 2, d), s3_recv.at[op, i, d])

    terms = subs * per_block

    def make_pick():
        row = lax.broadcasted_iota(jnp.int32, (256, 128), 0)
        for i in range(chunks):
            for h in range(2):
                for sub in range(subs):
                    lane = sub * per_block + 2 * i + h
                    one = (row == lane) | (row == terms + lane) | (row == 128 + lane)
                    at = (h * subs + sub) * 128
                    pick[i, :, at : at + 128] = jnp.where(one, 1.0, 0.0).astype(BF16)

    def split_scales(op):
        n = OWNERS * 8
        lane = lax.broadcasted_iota(jnp.int32, (n, 128), 1)
        for step in range(RING):
            both_sides = raw_s[op, step].reshape(n, 128)
            for side in range(2):
                s = pltpu.roll(both_sides, 128 - terms, 1) if side else both_sides
                s = jnp.where(lane < terms, s, 0.0)
                high = s.astype(BF16).astype(F32)
                middle = (s - high).astype(BF16).astype(F32)
                low = (s - high) - middle
                at = pl.ds((step * 2 + side) * n, n)
                split_s[op, at, :128] = (high + pltpu.roll(middle, terms, 1)).astype(BF16)
                split_s[op, at, 128:] = low.astype(BF16)

    def expand(op, i):
        for n in range(0, wide_s.shape[2], 256):
            wide_s[wide(op, i), :, n : n + 256] = jnp.dot(
                split_s[op], pick[i, :, n : n + 256], preferred_element_type=F32
            )

    def wide(op, i):
        ahead = i - (chunks - EARLY)
        return 1 + 2 * ahead + op if ahead >= 0 else 0

    def standardize(op, i):
        if i < chunks - EARLY:
            expand(op, i)

        def add(p, carry):
            sums, squares = list(carry[0]), list(carry[1])
            parts = [[], []]
            for q in range(OWNERS):
                block = raw[i, op, p // 2, p % 2, q].astype(F32)
                at = p * OWNERS + q
                if op == ADJ:
                    at = (q // 2) * 16 + (q % 2) * 8 + p
                part = pl.ds(pl.multiple_of(at * local_pair, 8), local_pair)
                s = pl.ds(pl.multiple_of((p * OWNERS + q) * 8, 8), 8)
                for h in range(2):
                    mine = [
                        block[n * 8 : n * 8 + 8] * wide_s[wide(op, i), s, n * 128 : n * 128 + 128]
                        for n in range(h * subs, (h + 1) * subs)
                    ]
                    work[part, h * HALF : (h + 1) * HALF] = jnp.concatenate(mine, axis=0)
                    parts[h] += mine
            for h in range(2):
                v = parts[h]
                w = [u * u for u in v]
                while len(v) > 1:
                    v = [sum(v[j : j + 2][1:], v[j]) for j in range(0, len(v), 2)]
                    w = [sum(w[j : j + 2][1:], w[j]) for j in range(0, len(w), 2)]
                sums[h] = sums[h] + v[0]
                squares[h] = squares[h] + w[0]
            return tuple(sums), tuple(squares)

        zero = jnp.zeros((8, HALF), F32)
        sums, squares = lax.fori_loop(
            0, CHIPS // OWNERS, add, ((zero, zero), (zero, zero)), unroll=2
        )
        average, factor = [], []
        for h in range(2):
            a = jnp.sum(sums[h], axis=0, keepdims=True) / tokens
            spread_ = jnp.sum(squares[h], axis=0, keepdims=True) / tokens - a * a
            average.append(a)
            factor.append(lax.rsqrt(spread_ + 1e-06) * (1.0 / math.sqrt(tokens)))

        rows = 128 if op == BASE else 96

        @pl.loop(0, tokens // rows, unroll=3 if op == BASE else 4)
        def _(t):
            part = pl.ds(pl.multiple_of(t * rows, rows), rows)
            for h in range(2):
                u = (work[part, h * HALF : (h + 1) * HALF] - average[h]) * factor[h]
                column = slice(i * CHUNK + h * HALF, i * CHUNK + (h + 1) * HALF)
                if op == BASE:
                    base_t[column, part] = u.astype(BF16).T
                else:
                    adj_u[core, part, column] = u.astype(BF16)

    swapped = set()

    traded = set()

    def depart(op, i):
        if op not in traded:
            traded.add(op)
            wait_for(peer_q.at[op], s0_recv.at[op])
            wait_for(peer_s.at[op], s0_recv.at[2 + op])
        if i < chunks:
            pack(op, i)
        else:
            pack_scales(op)
        scatter(op, i)

    def settle(op, i):
        arrived(op, i)
        if i == chunks:
            split_scales(op)
            return
        standardize(op, i)
        if op == ADJ:
            mine = adj_u.at[core, :, pl.ds(i * CHUNK, CHUNK)]
            remote(mine, mine, swap_send.at[i], swap_recv.at[i], peer).start()
        if i < EARLY:
            expand(op, chunks - 1 - i)

    def multiply(part, i):
        if i not in swapped:
            swapped.add(i)
            wait_for(adj_u.at[other, :, pl.ds(i * CHUNK, CHUNK)], swap_recv.at[i])

        @pl.loop(0, CORES)
        def _(half):
            (columns, rows)[part](base_t, adj_u, early, i, i * CHUNK, half)

    stage = {
        "d": depart, "e": exchange, "s": spread, "f": forward, "t": settle, "m": multiply,
    }
    for word in " ".join(ORDER).split():
        if word == "pick":
            make_pick()
        elif word != "m0b":
            stage[word[0]]("BA".index(word[2]) if word[0] != "m" else "ab".index(word[2]), int(word[1]))
    i = chunks - 1
    wait_for(adj_u.at[other, :, pl.ds(i * CHUNK, CHUNK)], swap_recv.at[i])

    for op in (BASE, ADJ):
        wait_for(peer_q.at[op], s0_send.at[op])
        wait_for(peer_s.at[op], s0_send.at[2 + op])
        for i in range(chunks + 1):
            wait_for(inbox(op, i).at[0, pl.ds(1, OWNERS - 1)], s1_send.at[op, i])
            wait_for(inbox(op, i).at[0], ex_send.at[op, i])
            for d in range(2):
                wait_for(slab(op, i, 0), s2_send.at[op, i, d])
                wait_for(half(op, i, 0, 0), s3_send.at[op, i, d])
    for i in range(chunks):
        wait_for(adj_u.at[core, :, pl.ds(i * CHUNK, CHUNK)], swap_send.at[i])


def gather(base_q, base_s, adj_q, adj_s):
    local, latents = base_q.shape
    width = latents // (OWNERS * CORES)
    chunks = width // CHUNK
    early = width - CHUNK
    tokens = local * CORES * RING**3
    rows = 2 * CORES * local
    subs = CORES * local // 8
    dma = pltpu.SemaphoreType.DMA
    whole = pl.BlockSpec(memory_space=VMEM)
    return pl.pallas_call(
        functools.partial(gather_kernel, local, width),
        out_shape=(
            VMEM((width, tokens), BF16),
            VMEM((CORES, tokens, width), BF16),
            VMEM((CORES, early, early), BF16),
        ),
        in_specs=[pl.BlockSpec(memory_space=pltpu.HBM)] * 4,
        out_specs=(whole,) * 3,
        scratch_shapes=[
            VMEM((2, OWNERS, local, width), BF16),
            VMEM((2,) + base_s.shape, F32),
            VMEM((2, OWNERS, local, width), BF16),
            VMEM((2,) + base_s.shape, F32),
            VMEM((chunks, 2, OWNERS, rows, HALF), BF16),
            VMEM((2, OWNERS, 8, 128), F32),
            VMEM((chunks, 2, RING, 2, OWNERS, rows, HALF), BF16),
            VMEM((2, 2, OWNERS, 8, 128), F32),
            VMEM((2, RING, OWNERS, 8, 128), F32),
            VMEM((2, CHIPS * 8, 256), BF16),
            VMEM((chunks, 256, 2 * subs * 128), BF16),
            VMEM((1 + 2 * EARLY, CHIPS * 8, 2 * subs * 128), F32),
            VMEM((tokens, CHUNK), F32),
            dma((2, OWNERS + 1)),
            dma((4,)), dma((4,)),
            dma((2, chunks + 1)), dma((2, chunks + 1)),
            dma((2, chunks + 1)), dma((2, chunks + 1)),
            dma((2, chunks + 1, 2)), dma((2, chunks + 1, 2)),
            dma((2, chunks + 1, 2)), dma((2, chunks + 1, 2)),
            dma((2, chunks + 1)),
            dma((chunks,)), dma((chunks,)),
        ],
        compiler_params=pltpu.CompilerParams(
            collective_id=0, has_side_effects=True, vmem_limit_bytes=32 << 20
        ),
        name="gather_units",
    )(base_q, base_s, adj_q, adj_s)


def product_kernel(base_t, adj_u, early, out, below, beside, early_sem, late_sem):
    width = base_t.shape[0]
    done_to = early.shape[1]
    moves = [
        pltpu.make_async_copy(
            early.at[half, a : a + CHUNK],
            out.at[a : a + CHUNK, half * width : half * width + done_to],
            early_sem.at[half, a // CHUNK],
        )
        for half in range(CORES)
        for a in range(0, done_to, CHUNK)
    ]
    for move in moves:
        move.start()

    def late(half, which):
        start = pl.multiple_of(half * width, width)
        if which == 0:
            at = out.at[:, pl.ds(start + done_to, CHUNK)]
            return pltpu.make_async_copy(below.at[half], at, late_sem.at[half, 0])
        at = out.at[pl.ds(done_to, CHUNK), pl.ds(start, done_to)]
        return pltpu.make_async_copy(beside.at[half], at, late_sem.at[half, 1])

    @pl.loop(0, CORES)
    def _(half):
        columns(base_t, adj_u, below, done_to // CHUNK, 0, half)
        late(half, 0).start()
        rows(base_t, adj_u, beside, done_to // CHUNK, 0, half)
        late(half, 1).start()

    for half in range(CORES):
        for which in range(2):
            late(half, which).wait()
    for move in moves:
        move.wait()


def product(base_t, adj_u, early):
    width = base_t.shape[0]
    whole = pl.BlockSpec(memory_space=VMEM)
    return pl.pallas_call(
        product_kernel,
        out_shape=jax.ShapeDtypeStruct((width, CORES * width), BF16),
        in_specs=[whole] * 3,
        out_specs=pl.BlockSpec(memory_space=pl.ANY),
        scratch_shapes=[
            VMEM((CORES, width, CHUNK), BF16),
            VMEM((CORES, CHUNK, width - CHUNK), BF16),
            pltpu.SemaphoreType.DMA((CORES, width // CHUNK - 1)),
            pltpu.SemaphoreType.DMA((CORES, 2)),
        ],
        compiler_params=pltpu.CompilerParams(vmem_limit_bytes=8 << 20),
        name="correlate",
    )(base_t, adj_u, early)


def on_device(*args):
    units = gather(*args)
    return product(*(pltpu.with_memory_space_constraint(u, VMEM) for u in units))


def solution(mesh):
    spec = P(("row", "col"), None)
    return jax.shard_map(
        on_device, mesh=mesh, in_specs=(spec,) * 4, out_specs=P("row", "col"), check_vma=False
    )
```
